32 devices in a mesh: prow: 4 (over x, core), pcol: 8 (over z, y).
Axes of the slice: x: 2, y: 2, z: 4, core: 2. Of those that a mesh axis runs over, the one named last changes fastest.
Arguments:
- blocks: bfloat16 [20480, 128, 128], P(('prow', 'pcol')), may hold values from -0.078125 to 0.078125
- row_index: int32 [20480], P(('prow', 'pcol')), may hold values from 0 to 511, as said below
- col_index: int32 [20480], P(('prow', 'pcol')), may hold values from 0 to 511, as said below
- send_tiles: int32 [512], P(('prow', 'pcol')), may hold values from 0 to 511, as said below
- lighting: bfloat16 [65536, 384], P(('prow', 'pcol')), may hold values from -6 to 6
- albedo: float32 [3, 65536], P(None, ('pcol', 'prow')), may hold values from 0.2 to 0.95
- emission: bfloat16 [65536, 384], P(('pcol', 'prow')), may hold values from -4 to 4
Outputs:
- radiance: bfloat16 [65536, 384], P(('pcol', 'prow'))
The draws below stay inside these ranges and needn't reach their ends.
Inputs may be any that keep to these rules, and one draw needn't show every extreme that they name: `send_tiles`: group g (the blocks of device g) lists 16 distinct tiles in increasing order: exactly 4 from each of the 4 ranges of 16 block rows starting at c * 64 + r * 16, r = 0 .. 3, where c = g % 8. `row_index`: each block's row is one of its group's listed tiles, each listed tile has at least one block, and a group's blocks are ordered by row; counts per tile are uneven. `col_index`: the blocks of group g have columns in (g // 8) * 128 to (g // 8 + 1) * 128 - 1; a pair of row and column may repeat, and then the blocks add.
All inputs are finite; a program needn't handle non-finite values.
Results may differ from the reference program's by a relative error of at most 0.008.
Values may be sent and summed in bfloat16 or wider, within the bound.
A program may use at most 192 MiB of HBM per device.

```python
import jax
import jax.numpy as jnp
from jax import lax

TILE = 128
COLORS = 3
BASIS = 128
OWN_TILES = 16
BLK_DEV = 640
SEND_OWN = 4
COLS = 384
NSEND = 16
NB = 512
NPATCH = 65536
BLOCKS = 20480
N_PROW = 4
N_PCOL = 8
DEVICES = 32


def pattern(key):
    device_ids = jnp.arange(DEVICES)
    prow_ids = device_ids // N_PCOL
    pcol_ids = device_ids % N_PCOL
    scores = jax.random.randint(jax.random.fold_in(key, 11), (DEVICES, N_PROW, OWN_TILES), 0, 1 << 20) * OWN_TILES + jnp.arange(OWN_TILES)
    chosen = jnp.sort(jnp.argsort(scores, axis=-1)[..., :SEND_OWN], axis=-1)
    local = jnp.arange(N_PROW)[None, :, None] * OWN_TILES + chosen
    listed = (pcol_ids[:, None, None] * (OWN_TILES * N_PROW) + local).reshape(DEVICES, NSEND)
    first = jax.random.randint(jax.random.fold_in(key, 12), (DEVICES, BLK_DEV), 0, NSEND)
    second = jax.random.randint(jax.random.fold_in(key, 13), (DEVICES, BLK_DEV), 0, NSEND)
    slots = first * second // NSEND
    positions = jnp.arange(BLK_DEV)[None, :]
    slots = jnp.where(positions < NSEND, positions, slots)
    slots = jnp.sort(slots, axis=-1)
    rows = jnp.take_along_axis(listed, slots, axis=1)
    offsets = jax.random.randint(jax.random.fold_in(key, 14), (DEVICES, BLK_DEV), 0, OWN_TILES * N_PCOL)
    columns = prow_ids[:, None] * (OWN_TILES * N_PCOL) + offsets
    return (listed.reshape(-1).astype(jnp.int32), rows.reshape(-1).astype(jnp.int32), columns.reshape(-1).astype(jnp.int32))


def draw_send_tiles(key, part):
    return pattern(key)[0]


def draw_row_index(key, part):
    return pattern(key)[1]


def draw_col_index(key, part):
    return pattern(key)[2]


def steps_of(own_key, shape, pieces, low, high):
    loudness = 1.0
    for axis_at, blocks in pieces:
        draws = jax.random.uniform(jax.random.fold_in(jax.random.fold_in(own_key, 6), axis_at), (blocks,), jnp.float32, low / len(pieces), high / len(pieces))
        loudness = loudness * jnp.repeat(jnp.exp(draws), shape[axis_at] // blocks).reshape((-1,) + (1,) * (len(shape) - 1 - axis_at))
    return loudness


def gaussian(stream_key, shape, scale, bound, cuts=(), dtype=jnp.bfloat16):
    drawn = jax.random.normal(stream_key, shape, jnp.float32) * scale
    if len(cuts) > 0:
        drawn = steps_of(stream_key, shape, cuts, -0.22, 0.18) * drawn
    return jnp.clip(drawn, min=-bound, max=bound).astype(dtype)


def setup_inputs(seed: int = 0) -> dict:
    splits = jax.random.split(jax.random.key(seed), 8)
    blocks = gaussian(splits[0], (BLOCKS, TILE, TILE), (TILE * BLK_DEV // OWN_TILES) ** -0.5, 0.078125, ((0, 32),))
    row_index = draw_row_index(jax.random.fold_in(splits[7], 71), 0)
    col_index = draw_col_index(jax.random.fold_in(splits[7], 71), 0)
    send_tiles = draw_send_tiles(jax.random.fold_in(splits[7], 71), 0)
    lighting = gaussian(splits[4], (NPATCH, COLS), 1.0, 6.0, ((0, 32),))
    albedo = jnp.clip(0.2 + 0.75 * jax.random.uniform(splits[5], (COLORS, NPATCH), jnp.float32) ** steps_of(splits[5], (COLORS, NPATCH), ((1, 32),), -0.2, 0.2), 0.2, 0.95)
    emission = gaussian(splits[6], (NPATCH, COLS), 0.5, 4.0, ((0, 32),))
    return dict(blocks=blocks, row_index=row_index, col_index=col_index, send_tiles=send_tiles, lighting=lighting, albedo=albedo, emission=emission)


def reference(blocks, row_index, col_index, send_tiles, lighting, albedo, emission):
    tiles = lighting.reshape(NB, TILE, COLS)
    grouped = blocks.reshape(DEVICES, BLK_DEV, TILE, TILE)
    rows = row_index.reshape(DEVICES, BLK_DEV).astype(jnp.int32)
    columns = col_index.reshape(DEVICES, BLK_DEV).astype(jnp.int32)
    listed = send_tiles.reshape(DEVICES, NSEND).astype(jnp.int32)

    def one_group(running, items):
        block_set, row_set, col_set, list_set = items
        slots = jnp.sum((list_set[None, :] < row_set[:, None]).astype(jnp.int32), axis=1)
        product = jnp.einsum("gpq,gqk->gpk", block_set.astype(jnp.float32), tiles[col_set].astype(jnp.float32))
        part = jax.ops.segment_sum(product, slots, num_segments=NSEND).astype(jnp.bfloat16)
        part = lax.optimization_barrier(part).astype(jnp.float32)
        return running.at[list_set].add(part), None

    start = jnp.zeros((NB, TILE, COLS), jnp.float32)
    gathered, _ = lax.scan(one_group, start, (grouped, rows, columns, listed))
    lit = gathered.reshape(NPATCH, COLORS, BASIS) * jnp.transpose(albedo)[:, :, None]
    return (lit.reshape(NPATCH, COLS) + emission.astype(jnp.float32)).astype(jnp.bfloat16)
```

```python
import functools

import jax
import jax.numpy as jnp
from jax import lax
from jax.experimental import pallas as pl
from jax.experimental.pallas import tpu as pltpu
from jax.sharding import PartitionSpec as P

GROUP = 8
BATCH = 12
LATE = 32
MESH = pl.DeviceIdType.MESH


def ring_place(pcol, n):
    odd = pcol % 2
    return (1 - odd) * (pcol // 2) + odd * (n - 1 - pcol // 2)


def ring_device(place, n):
    late = place // (n // 2)
    return (1 - late) * (2 * place) + late * (2 * (n - 1 - place) + 1)


def chunks_of(colours, tile):
    whole = [(c, 0, tile) for c in range(colours - 1)]
    return whole + [(colours - 1, 0, tile - LATE), (colours - 1, tile - LATE, LATE)]


def fused(
    n,
    rows,
    colours,
    groups,
    row_ref,
    col_ref,
    send_ref,
    blocks_ref,
    light_ref,
    albedo_ref,
    emission_ref,
    out_ref,
    *scratch,
):
    count, tile = blocks_ref.shape[:2]
    tiles = light_ref.shape[0]
    owned = emission_ref.shape[0]
    chunks = chunks_of(colours, tile)
    take = iter(scratch)
    slabs = [next(take) for _ in chunks]
    arrived = [next(take) for _ in range(colours)]
    lit = [next(take) for _ in range(colours)]
    parts = [next(take) for _ in range(2)]
    got = [next(take) for _ in range(rows)]
    (
        blk,
        packed,
        sums,
        alb_in,
        alb_rows,
        alb_cols,
        row_s,
        col_s,
        past_s,
        last_s,
        gsrc,
        gcol,
        keep_s,
        pos_s,
        ring_send,
        ring_recv,
        own_sem,
        blk_sem,
        index_sem,
        alb_sem,
        em_sem,
        out_sem,
        ex_send,
        ex_recv,
        ex_own,
        id_send,
        id_recv,
    ) = take
    half = tiles // 2
    listed = send_ref.shape[0]
    per = listed // rows
    basis = slabs[0].shape[2]
    batches = groups // BATCH
    prow = lax.axis_index("prow")
    pcol = lax.axis_index("pcol")
    place = ring_place(pcol, n)
    after = ring_device((place + 1) % n, n)
    before = ring_device((place + n - 1) % n, n)
    messages = n - 1

    barrier = pltpu.get_barrier_semaphore()
    for side in (after, before):
        pl.semaphore_signal(barrier, inc=1, device_id={"pcol": side}, device_id_type=MESH)
    for d in range(1, rows):
        pl.semaphore_signal(barrier, inc=1, device_id={"prow": (prow + d) % rows}, device_id_type=MESH)

    own = [
        pltpu.make_async_copy(
            light_ref.at[:, pl.ds(o, h), pl.ds(c * basis, basis)], slabs[k].at[pl.ds(pcol * tiles, tiles)], own_sem.at[k]
        )
        for k, (c, o, h) in enumerate(chunks)
    ]
    for copy in own:
        copy.start()
    loads = [
        pltpu.make_async_copy(row_ref, row_s, index_sem.at[0]),
        pltpu.make_async_copy(col_ref, col_s, index_sem.at[1]),
        pltpu.make_async_copy(send_ref, got[0], index_sem.at[2]),
    ]
    load = pltpu.make_async_copy(blocks_ref, blk.at[pl.ds(0, count)], blk_sem)
    load_albedo = pltpu.make_async_copy(albedo_ref, alb_in, alb_sem)
    load_emission = [
        pltpu.make_async_copy(emission_ref.at[:, :, pl.ds(c * basis, basis)], lit[c], em_sem.at[c]) for c in range(colours)
    ]
    store_out = [
        pltpu.make_async_copy(lit[c], out_ref.at[:, :, pl.ds(c * basis, basis)], out_sem.at[c]) for c in range(colours)
    ]
    pl.semaphore_wait(barrier, 2 + rows - 1)

    def piece(k, m, way, arriving):
        step = m // 2
        part = (m + way) % 2
        if way == 0:
            source = (place + n - step - arriving) % n
        else:
            source = (place + step + arriving) % n
        at = ring_device(source, n) * tiles + part * half
        window = slabs[k].at[pl.ds(at, half)]
        return pltpu.make_async_remote_copy(
            src_ref=window,
            dst_ref=window,
            send_sem=ring_send.at[way, k, m],
            recv_sem=ring_recv.at[way, k, m],
            device_id={"pcol": before if way else after},
            device_id_type=MESH,
        )

    def to_row(c, d):
        target = (prow + d) % rows
        return pltpu.make_async_remote_copy(
            src_ref=parts[c % 2].at[pl.ds(target * per, per)],
            dst_ref=arrived[c].at[pl.ds(prow * per, per)],
            send_sem=ex_send.at[c, d],
            recv_sem=ex_recv.at[c, d],
            device_id={"prow": target},
            device_id_type=MESH,
        )

    def from_row(c, d):
        origin = (prow + rows - d) % rows
        return pltpu.make_async_remote_copy(
            src_ref=parts[c % 2].at[pl.ds(0, per)],
            dst_ref=arrived[c].at[pl.ds(origin * per, per)],
            send_sem=ex_send.at[c, d],
            recv_sem=ex_recv.at[c, d],
            device_id={"prow": origin},
            device_id_type=MESH,
        )

    def stay(c):
        return pltpu.make_async_copy(
            parts[c % 2].at[pl.ds(prow * per, per)], arrived[c].at[pl.ds(prow * per, per)], ex_own.at[c]
        )

    def ids(d):
        return pltpu.make_async_remote_copy(
            src_ref=send_ref,
            dst_ref=got[d],
            send_sem=id_send.at[d],
            recv_sem=id_recv.at[d],
            device_id={"prow": (prow + d) % rows},
            device_id_type=MESH,
        )

    def start_loads():
        for copy in loads:
            copy.start()
        for d in range(1, rows):
            ids(d).start()
        load.start()
        load_albedo.start()
        for copy in load_emission:
            copy.start()

    def make_plan():
        for copy in loads:
            copy.wait()

        def slot(s, carry):
            first, end = carry
            wanted = got[0][s]

            def narrow(_, bounds):
                low, high = bounds
                middle = (low + high) // 2
                up = jnp.logical_and(low < high, row_s[jnp.minimum(middle, count - 1)] <= wanted)
                return jnp.where(up, middle + 1, low), jnp.where(up, high, middle)

            past, _ = lax.fori_loop(0, count.bit_length(), narrow, (first, jnp.int32(count)))
            end = end + (past - first + GROUP - 1) // GROUP
            past_s[s] = past
            last_s[s] = jnp.clip(end - 1, 0, groups - 1)
            return past, end

        lax.fori_loop(0, listed, slot, (jnp.int32(0), jnp.int32(0)))
        low_col = prow * (n * tiles)

        def group(i, carry):
            s, at, keep = carry
            end = past_s[jnp.minimum(s, listed - 1)]
            for j in range(GROUP):
                inside = at + j < end
                gsrc[i * GROUP + j] = jnp.where(inside, at + j, count)
                column = col_s[jnp.minimum(at + j, count - 1)] - low_col
                gcol[i * GROUP + j] = jnp.where(inside, jnp.clip(column, 0, n * tiles - 1), 0)
            keep_s[i] = keep
            done = at + GROUP >= end
            return (
                jnp.where(done, s + 1, s),
                jnp.minimum(at + GROUP, end),
                jnp.where(done, 0, 1),
            )

        lax.fori_loop(0, groups, group, (jnp.int32(0), jnp.int32(0), jnp.int32(0)))

    def make_places():
        for d in range(1, rows):
            ids(d).wait_send()
            ids(d).wait_recv()
        low_tile = (pcol * rows + prow) * owned

        def place_of(t, carry):
            for d in range(rows):
                origin = (prow + rows - d) % rows
                at = jnp.int32(listed)
                for k in range(per):
                    at = jnp.where(got[d][prow * per + k] == low_tile + t, origin * per + k, at)
                pos_s[t * rows + d] = at
            return carry

        lax.fori_loop(0, owned, place_of, jnp.int32(0))

    def make_albedo():
        load_albedo.wait()
        alb_rows[...] = jnp.zeros(alb_rows.shape, alb_rows.dtype)
        for c in range(colours):
            for t in range(owned):
                alb_rows[pl.ds(c * owned + t, 1), :] = alb_in[pl.ds(c, 1), pl.ds(t * tile, tile)]
        alb_cols[...] = jnp.transpose(alb_rows[...])

    def pack():
        each = tile // LATE
        lane = lax.broadcasted_iota(jnp.int32, (tile, tile), 1)

        def one(g, carry):
            for h in range(GROUP // each):
                joined = jnp.zeros((tile, tile), blk.dtype)
                for j in range(each):
                    block = blk[gsrc[g * GROUP + h * each + j]]
                    shift = (j * LATE + LATE) % tile
                    if shift:
                        block = jnp.concatenate([block[:, tile - shift :], block[:, : tile - shift]], axis=1)
                    mine = jnp.logical_and(lane >= j * LATE, lane < (j + 1) * LATE)
                    joined = jnp.where(mine, block, joined)
                packed[g, :, pl.ds(h * tile, tile)] = joined
            return carry

        lax.fori_loop(0, groups, one, jnp.int32(0))

    def full_operands(k, g):
        left, right = [], []
        for j in range(GROUP):
            left.append(blk[gsrc[g * GROUP + j]])
            lighting = slabs[k][gcol[g * GROUP + j]]
            if lighting.shape[0] < tile:
                fill = jnp.zeros((tile - lighting.shape[0], basis), lighting.dtype)
                lighting = jnp.concatenate([lighting, fill], axis=0)
            right.append(lighting)
        return jnp.concatenate(left, axis=1), jnp.concatenate(right, axis=0)

    def late_operands(k, g):
        right = [slabs[k][gcol[g * GROUP + j]] for j in range(GROUP)]
        return packed[g], jnp.concatenate(right, axis=0)

    def compute(operands, k, low, high, running):
        def one(i, running):
            products = []
            for u in range(BATCH):
                left, right = operands(k, i * BATCH + u)
                products.append(jnp.dot(left, right, preferred_element_type=jnp.float32))
            for u in range(BATCH):
                running = running * keep_s[i * BATCH + u].astype(jnp.float32) + products[u]
                sums[i * BATCH + u] = running.astype(sums.dtype)
            return running

        return lax.fori_loop(low, high, one, running)

    def collect(c, send, add):
        for d in list(range(rows // 2, rows)) + list(range(rows // 2)):
            target = (prow + d) % rows
            for j in range(per):
                s = target * per + j
                value = sums[last_s[s]]
                if add:
                    value = (parts[c % 2][s].astype(jnp.float32) + value.astype(jnp.float32)).astype(sums.dtype)
                parts[c % 2][s] = value
            if send:
                if d:
                    to_row(c, d).start()
                else:
                    stay(c).start()

    def finish(c):
        for d in range(1, rows):
            to_row(c, d).wait_send()
            from_row(c, d).wait_recv()
        stay(c).wait()
        load_emission[c].wait()
        for t in range(owned):
            total = arrived[c][pos_s[t * rows]].astype(jnp.float32)
            for d in range(1, rows):
                total = total + arrived[c][pos_s[t * rows + d]].astype(jnp.float32)
            scale = alb_cols[:, pl.ds(c * owned + t, 1)]
            lit[c][t] = (total * scale + lit[c][t].astype(jnp.float32)).astype(lit[c].dtype)
        store_out[c].start()

    final = len(chunks) - 1
    steps = min(messages - 1, batches)
    cuts = [batches * i // steps for i in range(steps + 1)]
    for k in range(len(chunks)):
        own[k].wait()
        running = jnp.zeros((tile, basis), jnp.float32)
        for m in range(messages):
            for way in (0, 1):
                if m >= 2:
                    piece(k, m - 2, way, 1).wait_recv()
                piece(k, m, way, 0).start()
            if k == 0:
                if m == 1:
                    start_loads()
                    blk[count] = jnp.zeros(blk.shape[1:], blk.dtype)
                    for c in range(colours):
                        arrived[c][listed] = jnp.zeros(arrived[c].shape[1:], arrived[c].dtype)
                    make_plan()
                if m == 2:
                    make_places()
                    make_albedo()
                if m == 3:
                    load.wait()
                    pack()
            elif m >= 1:
                if m == 1:
                    for last in range(max(messages - 2, 0), messages):
                        for way in (0, 1):
                            piece(k - 1, last, way, 1).wait_recv()
                if m <= steps:
                    running = compute(full_operands, k - 1, cuts[m - 1], cuts[m], running)
                if m == steps:
                    collect(chunks[k - 1][0], k < final, False)
                if m == max(steps - 1, 1) and k >= 2:
                    finish(k - 2)
    for m in range(messages):
        for k in range(final):
            for way in (0, 1):
                piece(k, m, way, 0).wait_send()
    for m in range(max(messages - 2, 0), messages):
        for way in (0, 1):
            piece(final, m, way, 1).wait_recv()
    compute(late_operands, final, 0, batches, jnp.zeros((tile, basis), jnp.float32))
    collect(colours - 1, True, True)
    for m in range(messages):
        for way in (0, 1):
            piece(final, m, way, 0).wait_send()
    finish(colours - 1)
    for c in range(colours):
        store_out[c].wait()


def per_device(blocks, row_index, col_index, send_tiles, lighting, albedo, emission):
    count, tile = blocks.shape[:2]
    width = lighting.shape[1]
    colours = albedo.shape[0]
    basis = width // colours
    listed = send_tiles.shape[0]
    rows = lax.axis_size("prow")
    n = lax.axis_size("pcol")
    tiles = lighting.shape[0] // tile
    owned = emission.shape[0] // tile
    groups = (count + listed * (GROUP - 1)) // GROUP
    groups = -(-groups // BATCH) * BATCH
    chunks = chunks_of(colours, tile)
    final = len(chunks)

    hbm = pl.BlockSpec(memory_space=pl.ANY)
    bf16, f32, i32 = jnp.bfloat16, jnp.float32, jnp.int32
    dma = pltpu.SemaphoreType.DMA
    scratch = [pltpu.VMEM((n * tiles, h, basis), bf16) for _, _, h in chunks]
    scratch += [pltpu.VMEM((listed + 1, tile, basis), bf16) for _ in range(colours)]
    scratch += [pltpu.VMEM((owned, tile, basis), bf16) for _ in range(colours)]
    scratch += [pltpu.VMEM((listed, tile, basis), bf16) for _ in range(2)]
    scratch += [pltpu.SMEM((listed,), i32) for _ in range(rows)]
    scratch += [
        pltpu.VMEM((count + 1, tile, tile), bf16),
        pltpu.VMEM((groups, tile, GROUP * LATE), bf16),
        pltpu.VMEM((groups, tile, basis), bf16),
        pltpu.VMEM((colours, owned * tile), f32),
        pltpu.VMEM((tile, tile), f32),
        pltpu.VMEM((tile, tile), f32),
        pltpu.SMEM((count,), i32),
        pltpu.SMEM((count,), i32),
        pltpu.SMEM((listed,), i32),
        pltpu.SMEM((listed,), i32),
        pltpu.SMEM((groups * GROUP,), i32),
        pltpu.SMEM((groups * GROUP,), i32),
        pltpu.SMEM((groups,), i32),
        pltpu.SMEM((owned * rows,), i32),
        dma((2, final, n - 1)),
        dma((2, final, n - 1)),
        dma((final,)),
        dma,
        dma((3,)),
        dma,
        dma((colours,)),
        dma((colours,)),
        dma((colours, rows)),
        dma((colours, rows)),
        dma((colours,)),
        dma((rows,)),
        dma((rows,)),
    ]
    tile_bytes = tile * basis * 2
    vmem = (count + 1) * tile * tile * 2 + groups * tile * (GROUP * LATE + basis) * 2
    vmem += (n * tiles * colours + (listed + 1 + owned) * colours + 2 * listed) * tile_bytes
    out = pl.pallas_call(
        functools.partial(fused, n, rows, colours, groups),
        out_shape=jax.ShapeDtypeStruct((owned, tile, width), bf16),
        in_specs=[hbm] * 7,
        out_specs=hbm,
        scratch_shapes=scratch,
        compiler_params=pltpu.CompilerParams(
            collective_id=0, has_side_effects=True, vmem_limit_bytes=max(vmem + (2 << 20), 58 << 20)
        ),
        cost_estimate=pl.CostEstimate(
            flops=2 * count * tile * tile * width,
            bytes_accessed=count * tile * tile * 2 + n * tiles * colours * tile_bytes,
            transcendentals=0,
        ),
    )(
        row_index,
        col_index,
        send_tiles,
        blocks,
        lighting.reshape(tiles, tile, width),
        albedo,
        emission.reshape(owned, tile, width),
    )
    return out.reshape(owned * tile, width)


def solution(mesh):
    placed = (
        P(("prow", "pcol"), None, None),
        P(("prow", "pcol")),
        P(("prow", "pcol")),
        P(("prow", "pcol")),
        P(("prow", "pcol"), None),
        P(None, ("pcol", "prow")),
        P(("pcol", "prow"), None),
    )
    return jax.shard_map(
        per_device, mesh=mesh, in_specs=placed, out_specs=P(("pcol", "prow"), None), check_vma=False
    )
```

```python
import functools

import jax
import jax.numpy as jnp
from jax import lax
from jax.experimental import pallas as pl
from jax.experimental.pallas import tpu as pltpu
from jax.sharding import PartitionSpec as P

GROUP = 8
BATCH = 12
MIB = 1 << 20
MESH = pl.DeviceIdType.MESH


def ring_place(pcol, n):
    odd = pcol % 2
    return (1 - odd) * (pcol // 2) + odd * (n - 1 - pcol // 2)


def ring_device(place, n):
    late = place // (n // 2)
    return (1 - late) * (2 * place) + late * (2 * (n - 1 - place) + 1)


def chunks_of(colours, tile, late):
    whole = [(c, 0, tile) for c in range(colours - 1)]
    return whole + [(colours - 1, 0, tile - late), (colours - 1, tile - late, late)]


def units_of(colours, tile):
    whole = [(c, 0, tile) for c in range(colours - 1)]
    return whole + [(colours - 1, 0, tile // 2), (colours - 1, tile // 2, tile // 2)]


def fused(
    n,
    rows,
    colours,
    groups,
    late,
    row_ref,
    col_ref,
    send_ref,
    blocks_ref,
    light_ref,
    albedo_ref,
    emission_ref,
    out_ref,
    *scratch,
):
    count, tile = blocks_ref.shape[:2]
    tiles = light_ref.shape[0]
    owned = emission_ref.shape[0]
    chunks = chunks_of(colours, tile, late)
    units = units_of(colours, tile)
    take = iter(scratch)
    slabs = [next(take) for _ in chunks]
    arrived = [next(take) for _ in units]
    lit = [next(take) for _ in range(colours)]
    parts = [next(take) for _ in range(2)]
    got = [next(take) for _ in range(rows)]
    (
        blk,
        packed,
        sums,
        alb_in,
        alb_rows,
        alb_cols,
        row_s,
        col_s,
        past_s,
        last_s,
        gsrc,
        gcol,
        keep_s,
        pos_s,
        ring_send,
        ring_recv,
        own_sem,
        blk_sem,
        index_sem,
        alb_sem,
        em_sem,
        out_sem,
        ex_send,
        ex_recv,
        ex_own,
        id_send,
        id_recv,
    ) = take
    half = tiles // 2
    listed = send_ref.shape[0]
    per = listed // rows
    basis = slabs[0].shape[2]
    batches = groups // BATCH
    prow = lax.axis_index("prow")
    pcol = lax.axis_index("pcol")
    place = ring_place(pcol, n)
    after = ring_device((place + 1) % n, n)
    before = ring_device((place + n - 1) % n, n)
    messages = n - 1

    barrier = pltpu.get_barrier_semaphore()
    for side in (after, before):
        pl.semaphore_signal(barrier, inc=1, device_id={"pcol": side}, device_id_type=MESH)
    for d in range(1, rows):
        pl.semaphore_signal(barrier, inc=1, device_id={"prow": (prow + d) % rows}, device_id_type=MESH)

    own = [
        pltpu.make_async_copy(
            light_ref.at[:, pl.ds(o, h), pl.ds(c * basis, basis)], slabs[k].at[pl.ds(pcol * tiles, tiles)], own_sem.at[k]
        )
        for k, (c, o, h) in enumerate(chunks)
    ]
    for copy in own:
        copy.start()
    loads = [
        pltpu.make_async_copy(row_ref, row_s, index_sem.at[0]),
        pltpu.make_async_copy(col_ref, col_s, index_sem.at[1]),
        pltpu.make_async_copy(send_ref, got[0], index_sem.at[2]),
    ]
    load = pltpu.make_async_copy(blocks_ref, blk.at[pl.ds(0, count)], blk_sem)
    load_albedo = pltpu.make_async_copy(albedo_ref, alb_in, alb_sem)
    load_emission = [
        pltpu.make_async_copy(emission_ref.at[:, :, pl.ds(c * basis, basis)], lit[c], em_sem.at[c]) for c in range(colours)
    ]
    store_out = [
        pltpu.make_async_copy(
            lit[c].at[:, pl.ds(o, h)], out_ref.at[:, pl.ds(o, h), pl.ds(c * basis, basis)], out_sem.at[u]
        )
        for u, (c, o, h) in enumerate(units)
    ]
    pl.semaphore_wait(barrier, 2 + rows - 1)

    def piece(k, m, way, arriving):
        step = m // 2
        part = (m + way) % 2
        if way == 0:
            source = (place + n - step - arriving) % n
        else:
            source = (place + step + arriving) % n
        at = ring_device(source, n) * tiles + part * half
        window = slabs[k].at[pl.ds(at, half)]
        return pltpu.make_async_remote_copy(
            src_ref=window,
            dst_ref=window,
            send_sem=ring_send.at[way, k, m],
            recv_sem=ring_recv.at[way, k, m],
            device_id={"pcol": before if way else after},
            device_id_type=MESH,
        )

    def to_row(u, d):
        c, o, h = units[u]
        target = (prow + d) % rows
        return pltpu.make_async_remote_copy(
            src_ref=parts[c % 2].at[pl.ds(target * per, per), pl.ds(o, h)],
            dst_ref=arrived[u].at[pl.ds(prow * per, per)],
            send_sem=ex_send.at[u, d],
            recv_sem=ex_recv.at[u, d],
            device_id={"prow": target},
            device_id_type=MESH,
        )

    def from_row(u, d):
        c, o, h = units[u]
        origin = (prow + rows - d) % rows
        return pltpu.make_async_remote_copy(
            src_ref=parts[c % 2].at[pl.ds(0, per), pl.ds(o, h)],
            dst_ref=arrived[u].at[pl.ds(origin * per, per)],
            send_sem=ex_send.at[u, d],
            recv_sem=ex_recv.at[u, d],
            device_id={"prow": origin},
            device_id_type=MESH,
        )

    def stay(u):
        c, o, h = units[u]
        return pltpu.make_async_copy(
            parts[c % 2].at[pl.ds(prow * per, per), pl.ds(o, h)], arrived[u].at[pl.ds(prow * per, per)], ex_own.at[u]
        )

    def ids(d):
        return pltpu.make_async_remote_copy(
            src_ref=send_ref,
            dst_ref=got[d],
            send_sem=id_send.at[d],
            recv_sem=id_recv.at[d],
            device_id={"prow": (prow + d) % rows},
            device_id_type=MESH,
        )

    def start_loads():
        for copy in loads:
            copy.start()
        for d in range(1, rows):
            ids(d).start()
        load.start()
        load_albedo.start()
        for copy in load_emission:
            copy.start()

    def make_plan():
        for copy in loads:
            copy.wait()

        def slot(s, carry):
            first, end = carry
            wanted = got[0][s]

            def narrow(_, bounds):
                low, high = bounds
                middle = (low + high) // 2
                up = jnp.logical_and(low < high, row_s[jnp.minimum(middle, count - 1)] <= wanted)
                return jnp.where(up, middle + 1, low), jnp.where(up, high, middle)

            past, _ = lax.fori_loop(0, count.bit_length(), narrow, (first, jnp.int32(count)))
            end = end + (past - first + GROUP - 1) // GROUP
            past_s[s] = past
            last_s[s] = jnp.clip(end - 1, 0, groups - 1)
            return past, end

        lax.fori_loop(0, listed, slot, (jnp.int32(0), jnp.int32(0)))
        low_col = prow * (n * tiles)

        def group(i, carry):
            s, at, keep = carry
            end = past_s[jnp.minimum(s, listed - 1)]
            for j in range(GROUP):
                inside = at + j < end
                gsrc[i * GROUP + j] = jnp.where(inside, at + j, count)
                column = col_s[jnp.minimum(at + j, count - 1)] - low_col
                gcol[i * GROUP + j] = jnp.where(inside, jnp.clip(column, 0, n * tiles - 1), 0)
            keep_s[i] = keep
            done = at + GROUP >= end
            return (
                jnp.where(done, s + 1, s),
                jnp.minimum(at + GROUP, end),
                jnp.where(done, 0, 1),
            )

        lax.fori_loop(0, groups, group, (jnp.int32(0), jnp.int32(0), jnp.int32(0)))

    def make_places():
        for d in range(1, rows):
            ids(d).wait_send()
            ids(d).wait_recv()
        low_tile = (pcol * rows + prow) * owned

        def place_of(t, carry):
            for d in range(rows):
                origin = (prow + rows - d) % rows
                at = jnp.int32(listed)
                for k in range(per):
                    at = jnp.where(got[d][prow * per + k] == low_tile + t, origin * per + k, at)
                pos_s[t * rows + d] = at
            return carry

        lax.fori_loop(0, owned, place_of, jnp.int32(0))

    def make_albedo():
        load_albedo.wait()
        alb_rows[...] = jnp.zeros(alb_rows.shape, alb_rows.dtype)
        for c in range(colours):
            for t in range(owned):
                alb_rows[pl.ds(c * owned + t, 1), :] = alb_in[pl.ds(c, 1), pl.ds(t * tile, tile)]
        alb_cols[...] = jnp.transpose(alb_rows[...])

    def pack(low, high):
        each = tile // late
        lane = lax.broadcasted_iota(jnp.int32, (tile, tile), 1)

        def one(g, carry):
            for h in range(GROUP // each):
                joined = jnp.zeros((tile, tile), blk.dtype)
                for j in range(each):
                    block = blk[gsrc[g * GROUP + h * each + j]]
                    shift = (j * late + late) % tile
                    if shift:
                        block = jnp.concatenate([block[:, tile - shift :], block[:, : tile - shift]], axis=1)
                    mine = jnp.logical_and(lane >= j * late, lane < (j + 1) * late)
                    joined = jnp.where(mine, block, joined)
                packed[g, :, pl.ds(h * tile, tile)] = joined
            return carry

        lax.fori_loop(low, high, one, jnp.int32(0))

    def full_operands(k, g):
        left, right = [], []
        for j in range(GROUP):
            left.append(blk[gsrc[g * GROUP + j]])
            lighting = slabs[k][gcol[g * GROUP + j]]
            if lighting.shape[0] < tile:
                fill = jnp.zeros((tile - lighting.shape[0], basis), lighting.dtype)
                lighting = jnp.concatenate([lighting, fill], axis=0)
            right.append(lighting)
        return jnp.concatenate(left, axis=1), jnp.concatenate(right, axis=0)

    def late_operands(k, g, o, h):
        right = [slabs[k][gcol[g * GROUP + j]] for j in range(GROUP)]
        return packed[g, pl.ds(o, h)], jnp.concatenate(right, axis=0)

    def compute(operands, batch, o, h, low, high, running):
        def one(i, running):
            products = []
            for b in range(batch):
                left, right = operands(i * batch + b)
                products.append(jnp.dot(left, right, preferred_element_type=jnp.float32))
            for b in range(batch):
                running = running * keep_s[i * batch + b].astype(jnp.float32) + products[b]
                sums[i * batch + b, pl.ds(o, h)] = running.astype(sums.dtype)
            return running

        return lax.fori_loop(low, high, one, running)

    def collect(c, o, h, add, u):
        for d in list(range(rows // 2, rows)) + list(range(rows // 2)):
            target = (prow + d) % rows
            for j in range(per):
                s = target * per + j
                value = sums[last_s[s], pl.ds(o, h)]
                if add:
                    before = parts[c % 2][s, pl.ds(o, h)]
                    value = (before.astype(jnp.float32) + value.astype(jnp.float32)).astype(sums.dtype)
                parts[c % 2][s, pl.ds(o, h)] = value
            if u is not None:
                if d:
                    to_row(u, d).start()
                else:
                    stay(u).start()

    def finish(u):
        c, o, h = units[u]
        for d in range(1, rows):
            to_row(u, d).wait_send()
            from_row(u, d).wait_recv()
        stay(u).wait()
        if o == 0:
            load_emission[c].wait()
        for t in range(owned):
            total = arrived[u][pos_s[t * rows]].astype(jnp.float32)
            for d in range(1, rows):
                total = total + arrived[u][pos_s[t * rows + d]].astype(jnp.float32)
            scale = alb_cols[pl.ds(o, h), pl.ds(c * owned + t, 1)]
            before = lit[c][t, pl.ds(o, h)].astype(jnp.float32)
            lit[c][t, pl.ds(o, h)] = (total * scale + before).astype(lit[c].dtype)
        store_out[u].start()

    final = len(chunks) - 1
    steps = min(messages - 1, batches)
    cuts = [batches * i // steps for i in range(steps + 1)]
    packs = [groups * i // (messages - 3) for i in range(messages - 2)]
    for k in range(len(chunks)):
        own[k].wait()
        running = jnp.zeros((tile, basis), jnp.float32)
        for m in range(messages):
            for way in (0, 1):
                if m >= 2:
                    piece(k, m - 2, way, 1).wait_recv()
                piece(k, m, way, 0).start()
            if k == 0:
                if m == 1:
                    start_loads()
                    blk[count] = jnp.zeros(blk.shape[1:], blk.dtype)
                    for buffer in arrived:
                        buffer[listed] = jnp.zeros(buffer.shape[1:], buffer.dtype)
                    make_plan()
                if m == 2:
                    make_places()
                    make_albedo()
                if m == 3:
                    load.wait()
                if m >= 3:
                    pack(packs[m - 3], packs[m - 2])
            elif m >= 1:
                if m == 1:
                    for last in range(max(messages - 2, 0), messages):
                        for way in (0, 1):
                            piece(k - 1, last, way, 1).wait_recv()
                if m <= steps:
                    operands = functools.partial(full_operands, k - 1)
                    running = compute(operands, BATCH, 0, tile, cuts[m - 1], cuts[m], running)
                if m == steps:
                    collect(chunks[k - 1][0], 0, tile, False, k - 1 if k < final else None)
                if m == max(steps - 1, 1) and k >= 2:
                    finish(k - 2)
                for way in (0, 1):
                    piece(k - 1, m, way, 0).wait_send()
                    if m == 1:
                        piece(k - 1, 0, way, 0).wait_send()
    for m in range(max(messages - 2, 0), messages):
        for way in (0, 1):
            piece(final, m, way, 1).wait_recv()
    batch = 2 * BATCH if batches % 2 == 0 else BATCH
    for u in range(colours - 1, len(units)):
        c, o, h = units[u]
        operands = functools.partial(late_operands, final, o=o, h=h)
        compute(operands, batch, o, h, 0, groups // batch, jnp.zeros((h, basis), jnp.float32))
        collect(c, o, h, True, u)
    for m in range(messages):
        for way in (0, 1):
            piece(final, m, way, 0).wait_send()
    for u in range(colours - 1, len(units)):
        finish(u)
    for copy in store_out:
        copy.wait()


def per_device(blocks, row_index, col_index, send_tiles, lighting, albedo, emission):
    count, tile = blocks.shape[:2]
    width = lighting.shape[1]
    colours = albedo.shape[0]
    basis = width // colours
    listed = send_tiles.shape[0]
    rows = lax.axis_size("prow")
    n = lax.axis_size("pcol")
    tiles = lighting.shape[0] // tile
    owned = emission.shape[0] // tile
    groups = (count + listed * (GROUP - 1)) // GROUP
    groups = -(-groups // BATCH) * BATCH
    units = units_of(colours, tile)

    def vmem_of(late):
        tall = n * tiles * colours + (listed + 1 + owned) * colours + 2 * listed + groups
        return ((count + 1) * tile * tile + groups * tile * GROUP * late + tall * tile * basis) * 2

    late = tile // 2 if vmem_of(tile // 2) <= 58 * MIB else tile // 4
    chunks = chunks_of(colours, tile, late)
    final = len(chunks)

    hbm = pl.BlockSpec(memory_space=pltpu.HBM)
    bf16, f32, i32 = jnp.bfloat16, jnp.float32, jnp.int32
    dma = pltpu.SemaphoreType.DMA
    scratch = [pltpu.VMEM((n * tiles, h, basis), bf16) for _, _, h in chunks]
    scratch += [pltpu.VMEM((listed + 1, h, basis), bf16) for _, _, h in units]
    scratch += [pltpu.VMEM((owned, tile, basis), bf16) for _ in range(colours)]
    scratch += [pltpu.VMEM((listed, tile, basis), bf16) for _ in range(2)]
    scratch += [pltpu.SMEM((listed,), i32) for _ in range(rows)]
    scratch += [
        pltpu.VMEM((count + 1, tile, tile), bf16),
        pltpu.VMEM((groups, tile, GROUP * late), bf16),
        pltpu.VMEM((groups, tile, basis), bf16),
        pltpu.VMEM((colours, owned * tile), f32),
        pltpu.VMEM((tile, tile), f32),
        pltpu.VMEM((tile, tile), f32),
        pltpu.SMEM((count,), i32),
        pltpu.SMEM((count,), i32),
        pltpu.SMEM((listed,), i32),
        pltpu.SMEM((listed,), i32),
        pltpu.SMEM((groups * GROUP,), i32),
        pltpu.SMEM((groups * GROUP,), i32),
        pltpu.SMEM((groups,), i32),
        pltpu.SMEM((owned * rows,), i32),
        dma((2, final, n - 1)),
        dma((2, final, n - 1)),
        dma((final,)),
        dma,
        dma((3,)),
        dma,
        dma((colours,)),
        dma((len(units),)),
        dma((len(units), rows)),
        dma((len(units), rows)),
        dma((len(units),)),
        dma((rows,)),
        dma((rows,)),
    ]
    tile_bytes = tile * basis * 2
    out = pl.pallas_call(
        functools.partial(fused, n, rows, colours, groups, late),
        out_shape=jax.ShapeDtypeStruct((owned, tile, width), bf16),
        in_specs=[hbm] * 7,
        out_specs=pl.BlockSpec(memory_space=pl.ANY),
        scratch_shapes=scratch,
        compiler_params=pltpu.CompilerParams(
            collective_id=0, has_side_effects=True, vmem_limit_bytes=max(vmem_of(late) + 2 * MIB, 58 * MIB)
        ),
        cost_estimate=pl.CostEstimate(
            flops=2 * count * tile * tile * width,
            bytes_accessed=count * tile * tile * 2 + n * tiles * colours * tile_bytes,
            transcendentals=0,
        ),
    )(
        row_index,
        col_index,
        send_tiles,
        blocks,
        lighting.reshape(tiles, tile, width),
        albedo,
        emission.reshape(owned, tile, width),
    )
    return out.reshape(owned * tile, width)


def solution(mesh):
    placed = (
        P(("prow", "pcol"), None, None),
        P(("prow", "pcol")),
        P(("prow", "pcol")),
        P(("prow", "pcol")),
        P(("prow", "pcol"), None),
        P(None, ("pcol", "prow")),
        P(("pcol", "prow"), None),
    )
    return jax.shard_map(
        per_device, mesh=mesh, in_specs=placed, out_specs=P(("pcol", "prow"), None), check_vma=False
    )
```

```python
import functools

import jax
import jax.numpy as jnp
from jax import lax
from jax.experimental import pallas as pl
from jax.experimental.pallas import tpu as pltpu
from jax.sharding import PartitionSpec as P

GROUP = 8
BATCH = 12
MIB = 1 << 20
MESH = pl.DeviceIdType.MESH


def ring_place(pcol, n):
    odd = pcol % 2
    return (1 - odd) * (pcol // 2) + odd * (n - 1 - pcol // 2)


def ring_device(place, n):
    late = place // (n // 2)
    return (1 - late) * (2 * place) + late * (2 * (n - 1 - place) + 1)


def chunks_of(colours, tile, late):
    whole = [(c, 0, tile) for c in range(colours - 1)]
    return whole + [(colours - 1, 0, tile - late), (colours - 1, tile - late, late)]


def units_of(colours, tile):
    whole = [(c, 0, tile) for c in range(colours - 1)]
    return whole + [(colours - 1, 0, tile // 2), (colours - 1, tile // 2, tile // 2)]


def fused(
    n,
    rows,
    colours,
    groups,
    late,
    row_ref,
    col_ref,
    send_ref,
    blocks_ref,
    light_ref,
    albedo_ref,
    emission_ref,
    out_ref,
    *scratch,
):
    count, tile = blocks_ref.shape[:2]
    tiles = light_ref.shape[0]
    owned = emission_ref.shape[0]
    chunks = chunks_of(colours, tile, late)
    units = units_of(colours, tile)
    take = iter(scratch)
    slabs = [next(take) for _ in chunks]
    arrived = [next(take) for _ in units]
    parts = [next(take) for _ in range(2)]
    got = [next(take) for _ in range(rows)]
    (
        blk,
        packed,
        sums,
        alb_in,
        alb_rows,
        alb_cols,
        row_s,
        col_s,
        past_s,
        last_s,
        gsrc,
        gcol,
        keep_s,
        pos_s,
        ring_send,
        ring_recv,
        own_sem,
        blk_sem,
        index_sem,
        alb_sem,
        em_sem,
        ex_send,
        ex_recv,
        ex_own,
        id_send,
        id_recv,
    ) = take
    half = tiles // 2
    listed = send_ref.shape[0]
    per = listed // rows
    basis = slabs[0].shape[2]
    batches = groups // BATCH
    prow = lax.axis_index("prow")
    pcol = lax.axis_index("pcol")
    place = ring_place(pcol, n)
    after = ring_device((place + 1) % n, n)
    before = ring_device((place + n - 1) % n, n)
    messages = n - 1

    barrier = pltpu.get_barrier_semaphore()
    for side in (after, before):
        pl.semaphore_signal(barrier, inc=1, device_id={"pcol": side}, device_id_type=MESH)
    for d in range(1, rows):
        pl.semaphore_signal(barrier, inc=1, device_id={"prow": (prow + d) % rows}, device_id_type=MESH)

    own = [
        pltpu.make_async_copy(
            light_ref.at[:, pl.ds(o, h), pl.ds(c * basis, basis)], slabs[k].at[pl.ds(pcol * tiles, tiles)], own_sem.at[k]
        )
        for k, (c, o, h) in enumerate(chunks)
    ]
    for copy in own:
        copy.start()
    loads = [
        pltpu.make_async_copy(row_ref, row_s, index_sem.at[0]),
        pltpu.make_async_copy(col_ref, col_s, index_sem.at[1]),
        pltpu.make_async_copy(send_ref, got[0], index_sem.at[2]),
    ]
    load = pltpu.make_async_copy(blocks_ref, blk.at[pl.ds(0, count)], blk_sem)
    load_albedo = pltpu.make_async_copy(albedo_ref, alb_in, alb_sem)
    load_emission = pltpu.make_async_copy(emission_ref, out_ref, em_sem)
    pl.semaphore_wait(barrier, 2 + rows - 1)

    def piece(k, m, way, arriving):
        step = m // 2
        part = (m + way) % 2
        if way == 0:
            source = (place + n - step - arriving) % n
        else:
            source = (place + step + arriving) % n
        at = ring_device(source, n) * tiles + part * half
        window = slabs[k].at[pl.ds(at, half)]
        return pltpu.make_async_remote_copy(
            src_ref=window,
            dst_ref=window,
            send_sem=ring_send.at[way, k, m],
            recv_sem=ring_recv.at[way, k, m],
            device_id={"pcol": before if way else after},
            device_id_type=MESH,
        )

    def to_row(u, d):
        c, o, h = units[u]
        target = (prow + d) % rows
        return pltpu.make_async_remote_copy(
            src_ref=parts[c % 2].at[pl.ds(target * per, per), pl.ds(o, h)],
            dst_ref=arrived[u].at[pl.ds(prow * per, per)],
            send_sem=ex_send.at[u, d],
            recv_sem=ex_recv.at[u, d],
            device_id={"prow": target},
            device_id_type=MESH,
        )

    def from_row(u, d):
        c, o, h = units[u]
        origin = (prow + rows - d) % rows
        return pltpu.make_async_remote_copy(
            src_ref=parts[c % 2].at[pl.ds(0, per), pl.ds(o, h)],
            dst_ref=arrived[u].at[pl.ds(origin * per, per)],
            send_sem=ex_send.at[u, d],
            recv_sem=ex_recv.at[u, d],
            device_id={"prow": origin},
            device_id_type=MESH,
        )

    def stay(u):
        c, o, h = units[u]
        return pltpu.make_async_copy(
            parts[c % 2].at[pl.ds(prow * per, per), pl.ds(o, h)], arrived[u].at[pl.ds(prow * per, per)], ex_own.at[u]
        )

    def ids(d):
        return pltpu.make_async_remote_copy(
            src_ref=send_ref,
            dst_ref=got[d],
            send_sem=id_send.at[d],
            recv_sem=id_recv.at[d],
            device_id={"prow": (prow + d) % rows},
            device_id_type=MESH,
        )

    def start_loads():
        for copy in loads:
            copy.start()
        for d in range(1, rows):
            ids(d).start()
        load.start()
        load_albedo.start()
        load_emission.start()

    def make_plan():
        for copy in loads:
            copy.wait()

        def slot(s, carry):
            first, end = carry
            wanted = got[0][s]

            def narrow(_, bounds):
                low, high = bounds
                middle = (low + high) // 2
                up = jnp.logical_and(low < high, row_s[jnp.minimum(middle, count - 1)] <= wanted)
                return jnp.where(up, middle + 1, low), jnp.where(up, high, middle)

            past, _ = lax.fori_loop(0, count.bit_length(), narrow, (first, jnp.int32(count)))
            end = end + (past - first + GROUP - 1) // GROUP
            past_s[s] = past
            last_s[s] = jnp.clip(end - 1, 0, groups - 1)
            return past, end

        lax.fori_loop(0, listed, slot, (jnp.int32(0), jnp.int32(0)))
        low_col = prow * (n * tiles)

        def group(i, carry):
            s, at, keep = carry
            end = past_s[jnp.minimum(s, listed - 1)]
            for j in range(GROUP):
                inside = at + j < end
                gsrc[i * GROUP + j] = jnp.where(inside, at + j, count)
                column = col_s[jnp.minimum(at + j, count - 1)] - low_col
                gcol[i * GROUP + j] = jnp.where(inside, jnp.clip(column, 0, n * tiles - 1), 0)
            keep_s[i] = keep
            done = at + GROUP >= end
            return (
                jnp.where(done, s + 1, s),
                jnp.minimum(at + GROUP, end),
                jnp.where(done, 0, 1),
            )

        lax.fori_loop(0, groups, group, (jnp.int32(0), jnp.int32(0), jnp.int32(0)))

    def make_places():
        for d in range(1, rows):
            ids(d).wait_send()
            ids(d).wait_recv()
        low_tile = (pcol * rows + prow) * owned

        def place_of(t, carry):
            for d in range(rows):
                origin = (prow + rows - d) % rows
                at = jnp.int32(listed)
                for k in range(per):
                    at = jnp.where(got[d][prow * per + k] == low_tile + t, origin * per + k, at)
                pos_s[t * rows + d] = at
            return carry

        lax.fori_loop(0, owned, place_of, jnp.int32(0))

    def make_albedo():
        load_albedo.wait()
        alb_rows[...] = jnp.zeros(alb_rows.shape, alb_rows.dtype)
        for c in range(colours):
            for t in range(owned):
                alb_rows[pl.ds(c * owned + t, 1), :] = alb_in[pl.ds(c, 1), pl.ds(t * tile, tile)]
        alb_cols[...] = jnp.transpose(alb_rows[...])

    def pack(low, high):
        each = tile // late
        lane = lax.broadcasted_iota(jnp.int32, (tile, tile), 1)

        def one(g, carry):
            for h in range(GROUP // each):
                joined = jnp.zeros((tile, tile), blk.dtype)
                for j in range(each):
                    block = blk[gsrc[g * GROUP + h * each + j]]
                    shift = (j * late + late) % tile
                    if shift:
                        block = jnp.concatenate([block[:, tile - shift :], block[:, : tile - shift]], axis=1)
                    mine = jnp.logical_and(lane >= j * late, lane < (j + 1) * late)
                    joined = jnp.where(mine, block, joined)
                packed[g, :, pl.ds(h * tile, tile)] = joined
            return carry

        lax.fori_loop(low, high, one, jnp.int32(0))

    def full_operands(k, g):
        left, right = [], []
        for j in range(GROUP):
            left.append(blk[gsrc[g * GROUP + j]])
            lighting = slabs[k][gcol[g * GROUP + j]]
            if lighting.shape[0] < tile:
                fill = jnp.zeros((tile - lighting.shape[0], basis), lighting.dtype)
                lighting = jnp.concatenate([lighting, fill], axis=0)
            right.append(lighting)
        return jnp.concatenate(left, axis=1), jnp.concatenate(right, axis=0)

    def late_operands(k, g, o, h):
        right = [slabs[k][gcol[g * GROUP + j]] for j in range(GROUP)]
        return packed[g, pl.ds(o, h)], jnp.concatenate(right, axis=0)

    def compute(operands, batch, o, h, low, high, running):
        def one(i, running):
            products = []
            for b in range(batch):
                left, right = operands(i * batch + b)
                products.append(jnp.dot(left, right, preferred_element_type=jnp.float32))
            for b in range(batch):
                running = running * keep_s[i * batch + b].astype(jnp.float32) + products[b]
                sums[i * batch + b, pl.ds(o, h)] = running.astype(sums.dtype)
            return running

        return lax.fori_loop(low, high, one, running)

    def collect(c, o, h, add, u):
        for d in list(range(rows // 2, rows)) + list(range(rows // 2)):
            target = (prow + d) % rows
            for j in range(per):
                s = target * per + j
                value = sums[last_s[s], pl.ds(o, h)]
                if add:
                    before = parts[c % 2][s, pl.ds(o, h)]
                    value = (before.astype(jnp.float32) + value.astype(jnp.float32)).astype(sums.dtype)
                parts[c % 2][s, pl.ds(o, h)] = value
            if u is not None:
                if d:
                    to_row(u, d).start()
                else:
                    stay(u).start()

    def finish(u):
        c, o, h = units[u]
        for d in range(1, rows):
            to_row(u, d).wait_send()
            from_row(u, d).wait_recv()
        stay(u).wait()
        if u == 0:
            load_emission.wait()
        lanes = pl.ds(c * basis, basis)
        for t in range(owned):
            total = arrived[u][pos_s[t * rows]].astype(jnp.float32)
            for d in range(1, rows):
                total = total + arrived[u][pos_s[t * rows + d]].astype(jnp.float32)
            scale = alb_cols[pl.ds(o, h), pl.ds(c * owned + t, 1)]
            before = out_ref[t, pl.ds(o, h), lanes].astype(jnp.float32)
            out_ref[t, pl.ds(o, h), lanes] = (total * scale + before).astype(out_ref.dtype)

    final = len(chunks) - 1
    steps = min(messages - 1, batches)
    cuts = [batches * i // steps for i in range(steps + 1)]
    packs = [groups * i // (messages - 3) for i in range(messages - 2)]
    for k in range(len(chunks)):
        own[k].wait()
        running = jnp.zeros((tile, basis), jnp.float32)
        for m in range(messages):
            for way in (0, 1):
                if m >= 2:
                    piece(k, m - 2, way, 1).wait_recv()
                piece(k, m, way, 0).start()
            if k == 0:
                if m == 1:
                    start_loads()
                    blk[count] = jnp.zeros(blk.shape[1:], blk.dtype)
                    for buffer in arrived:
                        buffer[listed] = jnp.zeros(buffer.shape[1:], buffer.dtype)
                    make_plan()
                if m == 2:
                    make_places()
                    make_albedo()
                if m == 3:
                    load.wait()
                if m >= 3:
                    pack(packs[m - 3], packs[m - 2])
            elif m >= 1:
                if m == 1:
                    for last in range(max(messages - 2, 0), messages):
                        for way in (0, 1):
                            piece(k - 1, last, way, 1).wait_recv()
                if m <= steps:
                    operands = functools.partial(full_operands, k - 1)
                    running = compute(operands, BATCH, 0, tile, cuts[m - 1], cuts[m], running)
                if m == steps:
                    collect(chunks[k - 1][0], 0, tile, False, k - 1 if k < final else None)
                if m == max(steps - 1, 1) and k >= 2:
                    finish(k - 2)
                for way in (0, 1):
                    piece(k - 1, m, way, 0).wait_send()
                    if m == 1:
                        piece(k - 1, 0, way, 0).wait_send()
    for m in range(max(messages - 2, 0), messages):
        for way in (0, 1):
            piece(final, m, way, 1).wait_recv()
    batch = 2 * BATCH if batches % 2 == 0 else BATCH
    for u in range(colours - 1, len(units)):
        c, o, h = units[u]
        operands = functools.partial(late_operands, final, o=o, h=h)
        compute(operands, batch, o, h, 0, groups // batch, jnp.zeros((h, basis), jnp.float32))
        collect(c, o, h, True, u)
    for m in range(messages):
        for way in (0, 1):
            piece(final, m, way, 0).wait_send()
    for u in range(colours - 1, len(units)):
        finish(u)


def write_out(from_ref, out_ref, sem):
    pieces = sem.shape[0]
    size = from_ref.shape[0] // pieces
    copies = [
        pltpu.make_async_copy(from_ref.at[pl.ds(i * size, size)], out_ref.at[pl.ds(i * size, size)], sem.at[i])
        for i in range(pieces)
    ]
    for copy in copies:
        copy.start()
    for copy in copies:
        copy.wait()


def per_device(blocks, row_index, col_index, send_tiles, lighting, albedo, emission):
    count, tile = blocks.shape[:2]
    width = lighting.shape[1]
    colours = albedo.shape[0]
    basis = width // colours
    listed = send_tiles.shape[0]
    rows = lax.axis_size("prow")
    n = lax.axis_size("pcol")
    tiles = lighting.shape[0] // tile
    owned = emission.shape[0] // tile
    groups = (count + listed * (GROUP - 1)) // GROUP
    groups = -(-groups // BATCH) * BATCH
    units = units_of(colours, tile)

    def vmem_of(late):
        tall = n * tiles * colours + (listed + 1) * colours + 2 * listed + groups
        return ((count + 1) * tile * tile + groups * tile * GROUP * late + tall * tile * basis) * 2

    late = tile // 2 if vmem_of(tile // 2) <= 58 * MIB else tile // 4
    chunks = chunks_of(colours, tile, late)
    final = len(chunks)

    hbm = pl.BlockSpec(memory_space=pltpu.HBM)
    bf16, f32, i32 = jnp.bfloat16, jnp.float32, jnp.int32
    dma = pltpu.SemaphoreType.DMA
    scratch = [pltpu.VMEM((n * tiles, h, basis), bf16) for _, _, h in chunks]
    scratch += [pltpu.VMEM((listed + 1, h, basis), bf16) for _, _, h in units]
    scratch += [pltpu.VMEM((listed, tile, basis), bf16) for _ in range(2)]
    scratch += [pltpu.SMEM((listed,), i32) for _ in range(rows)]
    scratch += [
        pltpu.VMEM((count + 1, tile, tile), bf16),
        pltpu.VMEM((groups, tile, GROUP * late), bf16),
        pltpu.VMEM((groups, tile, basis), bf16),
        pltpu.VMEM((colours, owned * tile), f32),
        pltpu.VMEM((tile, tile), f32),
        pltpu.VMEM((tile, tile), f32),
        pltpu.SMEM((count,), i32),
        pltpu.SMEM((count,), i32),
        pltpu.SMEM((listed,), i32),
        pltpu.SMEM((listed,), i32),
        pltpu.SMEM((groups * GROUP,), i32),
        pltpu.SMEM((groups * GROUP,), i32),
        pltpu.SMEM((groups,), i32),
        pltpu.SMEM((owned * rows,), i32),
        dma((2, final, n - 1)),
        dma((2, final, n - 1)),
        dma((final,)),
        dma,
        dma((3,)),
        dma,
        dma,
        dma((len(units), rows)),
        dma((len(units), rows)),
        dma((len(units),)),
        dma((rows,)),
        dma((rows,)),
    ]
    tile_bytes = tile * basis * 2
    out = pl.pallas_call(
        functools.partial(fused, n, rows, colours, groups, late),
        out_shape=pltpu.VMEM((owned, tile, width), bf16),
        in_specs=[hbm] * 7,
        out_specs=pl.BlockSpec(memory_space=pltpu.VMEM),
        scratch_shapes=scratch,
        compiler_params=pltpu.CompilerParams(
            collective_id=0, has_side_effects=True, vmem_limit_bytes=max(vmem_of(late) + MIB, 58 * MIB)
        ),
        cost_estimate=pl.CostEstimate(
            flops=2 * count * tile * tile * width,
            bytes_accessed=count * tile * tile * 2 + n * tiles * colours * tile_bytes,
            transcendentals=0,
        ),
    )(
        row_index,
        col_index,
        send_tiles,
        blocks,
        lighting.reshape(tiles, tile, width),
        albedo,
        emission.reshape(owned, tile, width),
    )
    out = pl.pallas_call(
        write_out,
        out_shape=jax.ShapeDtypeStruct((owned, tile, width), bf16),
        in_specs=[pl.BlockSpec(memory_space=pl.ANY)],
        out_specs=pl.BlockSpec(memory_space=pl.ANY),
        scratch_shapes=[dma((4,))],
        compiler_params=pltpu.CompilerParams(vmem_limit_bytes=8 * MIB),
    )(out)
    return out.reshape(owned * tile, width)


def solution(mesh):
    placed = (
        P(("prow", "pcol"), None, None),
        P(("prow", "pcol")),
        P(("prow", "pcol")),
        P(("prow", "pcol")),
        P(("prow", "pcol"), None),
        P(None, ("pcol", "prow")),
        P(("pcol", "prow"), None),
    )
    return jax.shard_map(
        per_device, mesh=mesh, in_specs=placed, out_specs=P(("pcol", "prow"), None), check_vma=False
    )
```

```python
import functools

import jax
import jax.numpy as jnp
from jax import lax
from jax.experimental import pallas as pl
from jax.experimental.pallas import tpu as pltpu
from jax.sharding import PartitionSpec as P

GROUP = 8
BATCH = 12
MIB = 1 << 20
MESH = pl.DeviceIdType.MESH


def ring_place(pcol, n):
    odd = pcol % 2
    return (1 - odd) * (pcol // 2) + odd * (n - 1 - pcol // 2)


def ring_device(place, n):
    late = place // (n // 2)
    return (1 - late) * (2 * place) + late * (2 * (n - 1 - place) + 1)


def chunks_of(colours, tile, late):
    whole = [(c, 0, tile) for c in range(colours - 1)]
    return whole + [(colours - 1, 0, tile - late), (colours - 1, tile - late, late)]


def units_of(colours, tile):
    whole = [(c, 0, tile) for c in range(colours - 1)]
    return whole + [(colours - 1, 0, tile // 2), (colours - 1, tile // 2, tile // 2)]


def fused(
    n,
    rows,
    colours,
    groups,
    late,
    row_ref,
    col_ref,
    send_ref,
    blocks_ref,
    light_ref,
    albedo_ref,
    emission_ref,
    out_ref,
    *scratch,
):
    count, tile = blocks_ref.shape[:2]
    tiles = light_ref.shape[0]
    owned = emission_ref.shape[0]
    chunks = chunks_of(colours, tile, late)
    units = units_of(colours, tile)
    take = iter(scratch)
    slabs = [next(take) for _ in chunks]
    arrived = [next(take) for _ in units]
    parts = [next(take) for _ in range(2)]
    got = [next(take) for _ in range(rows)]
    (
        blk,
        packed,
        sums,
        alb_in,
        alb_rows,
        alb_cols,
        row_s,
        col_s,
        past_s,
        last_s,
        gsrc,
        gcol,
        keep_s,
        pos_s,
        ring_send,
        ring_recv,
        own_sem,
        blk_sem,
        index_sem,
        alb_sem,
        em_sem,
        ex_send,
        ex_recv,
        ex_own,
        id_send,
        id_recv,
    ) = take
    half = tiles // 2
    listed = send_ref.shape[0]
    per = listed // rows
    basis = slabs[0].shape[2]
    batches = groups // BATCH
    prow = lax.axis_index("prow")
    pcol = lax.axis_index("pcol")
    place = ring_place(pcol, n)
    after = ring_device((place + 1) % n, n)
    before = ring_device((place + n - 1) % n, n)
    messages = n - 1

    barrier = pltpu.get_barrier_semaphore()
    for side in (after, before):
        pl.semaphore_signal(barrier, inc=1, device_id={"pcol": side}, device_id_type=MESH)
    for d in range(1, rows):
        pl.semaphore_signal(barrier, inc=1, device_id={"prow": (prow + d) % rows}, device_id_type=MESH)

    own = [
        pltpu.make_async_copy(
            light_ref.at[:, pl.ds(o, h), pl.ds(c * basis, basis)], slabs[k].at[pl.ds(pcol * tiles, tiles)], own_sem.at[k]
        )
        for k, (c, o, h) in enumerate(chunks)
    ]
    for copy in own:
        copy.start()
    loads = [
        pltpu.make_async_copy(row_ref, row_s, index_sem.at[0]),
        pltpu.make_async_copy(col_ref, col_s, index_sem.at[1]),
        pltpu.make_async_copy(send_ref, got[0], index_sem.at[2]),
    ]
    load = pltpu.make_async_copy(blocks_ref, blk.at[pl.ds(0, count)], blk_sem)
    load_albedo = pltpu.make_async_copy(albedo_ref, alb_in, alb_sem)
    load_emission = pltpu.make_async_copy(emission_ref, out_ref, em_sem)
    pl.semaphore_wait(barrier, 2 + rows - 1)

    def piece(k, m, way, arriving):
        step = m // 2
        part = (m + way) % 2
        if way == 0:
            source = (place + n - step - arriving) % n
        else:
            source = (place + step + arriving) % n
        at = ring_device(source, n) * tiles + part * half
        window = slabs[k].at[pl.ds(at, half)]
        return pltpu.make_async_remote_copy(
            src_ref=window,
            dst_ref=window,
            send_sem=ring_send.at[way, k, m],
            recv_sem=ring_recv.at[way, k, m],
            device_id={"pcol": before if way else after},
            device_id_type=MESH,
        )

    def to_row(u, d):
        c, o, h = units[u]
        target = (prow + d) % rows
        return pltpu.make_async_remote_copy(
            src_ref=parts[c % 2].at[pl.ds(target * per, per), pl.ds(o, h)],
            dst_ref=arrived[u].at[pl.ds(prow * per, per)],
            send_sem=ex_send.at[u, d],
            recv_sem=ex_recv.at[u, d],
            device_id={"prow": target},
            device_id_type=MESH,
        )

    def from_row(u, d):
        c, o, h = units[u]
        origin = (prow + rows - d) % rows
        return pltpu.make_async_remote_copy(
            src_ref=parts[c % 2].at[pl.ds(0, per), pl.ds(o, h)],
            dst_ref=arrived[u].at[pl.ds(origin * per, per)],
            send_sem=ex_send.at[u, d],
            recv_sem=ex_recv.at[u, d],
            device_id={"prow": origin},
            device_id_type=MESH,
        )

    def stay(u):
        c, o, h = units[u]
        return pltpu.make_async_copy(
            parts[c % 2].at[pl.ds(prow * per, per), pl.ds(o, h)], arrived[u].at[pl.ds(prow * per, per)], ex_own.at[u]
        )

    def ids(d):
        return pltpu.make_async_remote_copy(
            src_ref=send_ref,
            dst_ref=got[d],
            send_sem=id_send.at[d],
            recv_sem=id_recv.at[d],
            device_id={"prow": (prow + d) % rows},
            device_id_type=MESH,
        )

    def start_loads():
        for copy in loads:
            copy.start()
        for d in range(1, rows):
            ids(d).start()
        load.start()
        load_albedo.start()
        load_emission.start()

    def make_plan():
        for copy in loads:
            copy.wait()

        def slot(s, carry):
            first, end = carry
            wanted = got[0][s]

            def narrow(_, bounds):
                low, high = bounds
                middle = (low + high) // 2
                up = jnp.logical_and(low < high, row_s[jnp.minimum(middle, count - 1)] <= wanted)
                return jnp.where(up, middle + 1, low), jnp.where(up, high, middle)

            past, _ = lax.fori_loop(0, count.bit_length(), narrow, (first, jnp.int32(count)))
            end = end + (past - first + GROUP - 1) // GROUP
            past_s[s] = past
            last_s[s] = jnp.clip(end - 1, 0, groups - 1)
            return past, end

        lax.fori_loop(0, listed, slot, (jnp.int32(0), jnp.int32(0)))
        low_col = prow * (n * tiles)

        def group(i, carry):
            s, at, keep = carry
            end = past_s[jnp.minimum(s, listed - 1)]
            for j in range(GROUP):
                inside = at + j < end
                gsrc[i * GROUP + j] = jnp.where(inside, at + j, count)
                column = col_s[jnp.minimum(at + j, count - 1)] - low_col
                gcol[i * GROUP + j] = jnp.where(inside, jnp.clip(column, 0, n * tiles - 1), 0)
            keep_s[i] = keep
            done = at + GROUP >= end
            return (
                jnp.where(done, s + 1, s),
                jnp.minimum(at + GROUP, end),
                jnp.where(done, 0, 1),
            )

        lax.fori_loop(0, groups, group, (jnp.int32(0), jnp.int32(0), jnp.int32(0)))

    def make_places():
        for d in range(1, rows):
            ids(d).wait_send()
            ids(d).wait_recv()
        low_tile = (pcol * rows + prow) * owned

        def place_of(t, carry):
            for d in range(rows):
                origin = (prow + rows - d) % rows
                at = jnp.int32(listed)
                for k in range(per):
                    at = jnp.where(got[d][prow * per + k] == low_tile + t, origin * per + k, at)
                pos_s[t * rows + d] = at
            return carry

        lax.fori_loop(0, owned, place_of, jnp.int32(0))

    def make_albedo():
        load_albedo.wait()
        alb_rows[...] = jnp.zeros(alb_rows.shape, alb_rows.dtype)
        for c in range(colours):
            for t in range(owned):
                alb_rows[pl.ds(c * owned + t, 1), :] = alb_in[pl.ds(c, 1), pl.ds(t * tile, tile)]
        alb_cols[...] = jnp.transpose(alb_rows[...])

    def pack(low, high):
        each = tile // late
        lane = lax.broadcasted_iota(jnp.int32, (tile, tile), 1)

        def one(g, carry):
            for h in range(GROUP // each):
                joined = jnp.zeros((tile, tile), blk.dtype)
                for j in range(each):
                    block = blk[gsrc[g * GROUP + h * each + j]]
                    shift = (j * late + late) % tile
                    if shift:
                        block = jnp.concatenate([block[:, tile - shift :], block[:, : tile - shift]], axis=1)
                    mine = jnp.logical_and(lane >= j * late, lane < (j + 1) * late)
                    joined = jnp.where(mine, block, joined)
                packed[g, :, pl.ds(h * tile, tile)] = joined
            return carry

        lax.fori_loop(low, high, one, jnp.int32(0))

    def full_operands(k, g):
        left, right = [], []
        for j in range(GROUP):
            left.append(blk[gsrc[g * GROUP + j]])
            lighting = slabs[k][gcol[g * GROUP + j]]
            if lighting.shape[0] < tile:
                fill = jnp.zeros((tile - lighting.shape[0], basis), lighting.dtype)
                lighting = jnp.concatenate([lighting, fill], axis=0)
            right.append(lighting)
        return jnp.concatenate(left, axis=1), jnp.concatenate(right, axis=0)

    def late_operands(k, g, o, h):
        right = [slabs[k][gcol[g * GROUP + j]] for j in range(GROUP)]
        return packed[g, pl.ds(o, h)], jnp.concatenate(right, axis=0)

    def compute(operands, batch, o, h, low, high, running):
        def one(i, running):
            products = []
            for b in range(batch):
                left, right = operands(i * batch + b)
                products.append(jnp.dot(left, right, preferred_element_type=jnp.float32))
            for b in range(batch):
                running = running * keep_s[i * batch + b].astype(jnp.float32) + products[b]
                sums[i * batch + b, pl.ds(o, h)] = running.astype(sums.dtype)
            return running

        return lax.fori_loop(low, high, one, running)

    def collect(c, o, h, add, u):
        for d in list(range(rows // 2, rows)) + list(range(rows // 2)):
            target = (prow + d) % rows
            for j in range(per):
                s = target * per + j
                value = sums[last_s[s], pl.ds(o, h)]
                if add:
                    before = parts[c % 2][s, pl.ds(o, h)]
                    value = (before.astype(jnp.float32) + value.astype(jnp.float32)).astype(sums.dtype)
                parts[c % 2][s, pl.ds(o, h)] = value
            if u is not None:
                if d:
                    to_row(u, d).start()
                else:
                    stay(u).start()

    def finish(u):
        c, o, h = units[u]
        for d in range(1, rows):
            to_row(u, d).wait_send()
            from_row(u, d).wait_recv()
        stay(u).wait()
        if u == 0:
            load_emission.wait()
        lanes = pl.ds(c * basis, basis)
        for t in range(owned):
            total = arrived[u][pos_s[t * rows]].astype(jnp.float32)
            for d in range(1, rows):
                total = total + arrived[u][pos_s[t * rows + d]].astype(jnp.float32)
            scale = alb_cols[pl.ds(o, h), pl.ds(c * owned + t, 1)]
            before = out_ref[t, pl.ds(o, h), lanes].astype(jnp.float32)
            out_ref[t, pl.ds(o, h), lanes] = (total * scale + before).astype(out_ref.dtype)

    final = len(chunks) - 1
    steps = min(messages - 1, batches)
    cuts = [batches * i // steps for i in range(steps + 1)]
    packs = [groups * i // (messages - 3) for i in range(messages - 2)]
    for k in range(len(chunks)):
        own[k].wait()
        running = jnp.zeros((tile, basis), jnp.float32)
        for m in range(messages):
            for way in (0, 1):
                if m >= 2:
                    piece(k, m - 2, way, 1).wait_recv()
                piece(k, m, way, 0).start()
            if k == 0:
                if m == 1:
                    start_loads()
                    blk[count] = jnp.zeros(blk.shape[1:], blk.dtype)
                    for buffer in arrived:
                        buffer[listed] = jnp.zeros(buffer.shape[1:], buffer.dtype)
                    make_plan()
                if m == 2:
                    make_places()
                    make_albedo()
                if m == 3:
                    load.wait()
                if m >= 3:
                    pack(packs[m - 3], packs[m - 2])
            elif m >= 1:
                if m == 1:
                    for last in range(max(messages - 2, 0), messages):
                        for way in (0, 1):
                            piece(k - 1, last, way, 1).wait_recv()
                if m <= steps:
                    operands = functools.partial(full_operands, k - 1)
                    running = compute(operands, BATCH, 0, tile, cuts[m - 1], cuts[m], running)
                if m == steps:
                    collect(chunks[k - 1][0], 0, tile, False, k - 1 if k < final else None)
                if m == max(steps - 1, 1) and k >= 2:
                    finish(k - 2)
                for way in (0, 1):
                    piece(k - 1, m, way, 0).wait_send()
                    if m == 1:
                        piece(k - 1, 0, way, 0).wait_send()
    for m in range(max(messages - 2, 0), messages):
        for way in (0, 1):
            piece(final, m, way, 1).wait_recv()
    batch = max(b * BATCH for b in (1, 2, 4) if batches % b == 0)
    for u in range(colours - 1, len(units)):
        c, o, h = units[u]
        operands = functools.partial(late_operands, final, o=o, h=h)
        compute(operands, batch, o, h, 0, groups // batch, jnp.zeros((h, basis), jnp.float32))
        collect(c, o, h, True, u)
    for m in range(messages):
        for way in (0, 1):
            piece(final, m, way, 0).wait_send()
    for u in range(colours - 1, len(units)):
        finish(u)


def write_out(from_ref, out_ref, sem):
    pieces = sem.shape[0]
    size = from_ref.shape[0] // pieces
    copies = [
        pltpu.make_async_copy(from_ref.at[pl.ds(i * size, size)], out_ref.at[pl.ds(i * size, size)], sem.at[i])
        for i in range(pieces)
    ]
    for copy in copies:
        copy.start()
    for copy in copies:
        copy.wait()


def per_device(blocks, row_index, col_index, send_tiles, lighting, albedo, emission):
    count, tile = blocks.shape[:2]
    width = lighting.shape[1]
    colours = albedo.shape[0]
    basis = width // colours
    listed = send_tiles.shape[0]
    rows = lax.axis_size("prow")
    n = lax.axis_size("pcol")
    tiles = lighting.shape[0] // tile
    owned = emission.shape[0] // tile
    groups = (count + listed * (GROUP - 1)) // GROUP
    groups = -(-groups // BATCH) * BATCH
    units = units_of(colours, tile)

    def vmem_of(late):
        tall = n * tiles * colours + (listed + 1) * colours + 2 * listed + groups
        return ((count + 1) * tile * tile + groups * tile * GROUP * late + tall * tile * basis) * 2

    late = tile // 2 if vmem_of(tile // 2) <= 58 * MIB else tile // 4
    chunks = chunks_of(colours, tile, late)
    final = len(chunks)

    hbm = pl.BlockSpec(memory_space=pltpu.HBM)
    bf16, f32, i32 = jnp.bfloat16, jnp.float32, jnp.int32
    dma = pltpu.SemaphoreType.DMA
    scratch = [pltpu.VMEM((n * tiles, h, basis), bf16) for _, _, h in chunks]
    scratch += [pltpu.VMEM((listed + 1, h, basis), bf16) for _, _, h in units]
    scratch += [pltpu.VMEM((listed, tile, basis), bf16) for _ in range(2)]
    scratch += [pltpu.SMEM((listed,), i32) for _ in range(rows)]
    scratch += [
        pltpu.VMEM((count + 1, tile, tile), bf16),
        pltpu.VMEM((groups, tile, GROUP * late), bf16),
        pltpu.VMEM((groups, tile, basis), bf16),
        pltpu.VMEM((colours, owned * tile), f32),
        pltpu.VMEM((tile, tile), f32),
        pltpu.VMEM((tile, tile), f32),
        pltpu.SMEM((count,), i32),
        pltpu.SMEM((count,), i32),
        pltpu.SMEM((listed,), i32),
        pltpu.SMEM((listed,), i32),
        pltpu.SMEM((groups * GROUP,), i32),
        pltpu.SMEM((groups * GROUP,), i32),
        pltpu.SMEM((groups,), i32),
        pltpu.SMEM((owned * rows,), i32),
        dma((2, final, n - 1)),
        dma((2, final, n - 1)),
        dma((final,)),
        dma,
        dma((3,)),
        dma,
        dma,
        dma((len(units), rows)),
        dma((len(units), rows)),
        dma((len(units),)),
        dma((rows,)),
        dma((rows,)),
    ]
    tile_bytes = tile * basis * 2
    out = pl.pallas_call(
        functools.partial(fused, n, rows, colours, groups, late),
        out_shape=pltpu.VMEM((owned, tile, width), bf16),
        in_specs=[hbm] * 7,
        out_specs=pl.BlockSpec(memory_space=pltpu.VMEM),
        scratch_shapes=scratch,
        compiler_params=pltpu.CompilerParams(
            collective_id=0, has_side_effects=True, vmem_limit_bytes=max(vmem_of(late) + MIB, 58 * MIB)
        ),
        cost_estimate=pl.CostEstimate(
            flops=2 * count * tile * tile * width,
            bytes_accessed=count * tile * tile * 2 + n * tiles * colours * tile_bytes,
            transcendentals=0,
        ),
    )(
        row_index,
        col_index,
        send_tiles,
        blocks,
        lighting.reshape(tiles, tile, width),
        albedo,
        emission.reshape(owned, tile, width),
    )
    out = pl.pallas_call(
        write_out,
        out_shape=jax.ShapeDtypeStruct((owned, tile, width), bf16),
        in_specs=[pl.BlockSpec(memory_space=pl.ANY)],
        out_specs=pl.BlockSpec(memory_space=pl.ANY),
        scratch_shapes=[dma((4,))],
        compiler_params=pltpu.CompilerParams(vmem_limit_bytes=8 * MIB),
    )(out)
    return out.reshape(owned * tile, width)


def solution(mesh):
    placed = (
        P(("prow", "pcol"), None, None),
        P(("prow", "pcol")),
        P(("prow", "pcol")),
        P(("prow", "pcol")),
        P(("prow", "pcol"), None),
        P(None, ("pcol", "prow")),
        P(("pcol", "prow"), None),
    )
    return jax.shard_map(
        per_device, mesh=mesh, in_specs=placed, out_specs=P(("pcol", "prow"), None), check_vma=False
    )
```

```python
import functools

import jax
import jax.numpy as jnp
from jax import lax
from jax.experimental import pallas as pl
from jax.experimental.pallas import tpu as pltpu
from jax.sharding import PartitionSpec as P

GROUP = 8
BATCH = 12
MIB = 1 << 20
MESH = pl.DeviceIdType.MESH


def ring_place(pcol, n):
    odd = pcol % 2
    return (1 - odd) * (pcol // 2) + odd * (n - 1 - pcol // 2)


def ring_device(place, n):
    late = place // (n // 2)
    return (1 - late) * (2 * place) + late * (2 * (n - 1 - place) + 1)


def chunks_of(colours, tile, late):
    whole = [(c, 0, tile) for c in range(colours - 1)]
    return whole + [(colours - 1, 0, tile - late), (colours - 1, tile - late, late)]


def units_of(colours, tile):
    whole = [(c, 0, tile) for c in range(colours - 1)]
    return whole + [(colours - 1, 0, tile * 5 // 8), (colours - 1, tile * 5 // 8, tile * 3 // 8)]


def fused(
    n,
    rows,
    colours,
    groups,
    late,
    row_ref,
    col_ref,
    send_ref,
    blocks_ref,
    light_ref,
    albedo_ref,
    emission_ref,
    out_ref,
    *scratch,
):
    count, tile = blocks_ref.shape[:2]
    tiles = light_ref.shape[0]
    owned = emission_ref.shape[0]
    chunks = chunks_of(colours, tile, late)
    units = units_of(colours, tile)
    take = iter(scratch)
    slabs = [next(take) for _ in chunks]
    arrived = [next(take) for _ in units]
    parts = [next(take) for _ in range(2)]
    got = [next(take) for _ in range(rows)]
    (
        blk,
        packed,
        sums,
        alb_in,
        alb_rows,
        alb_cols,
        row_s,
        col_s,
        past_s,
        last_s,
        gsrc,
        gcol,
        keep_s,
        pos_s,
        ring_send,
        ring_recv,
        own_sem,
        blk_sem,
        index_sem,
        alb_sem,
        em_sem,
        ex_send,
        ex_recv,
        ex_own,
        id_send,
        id_recv,
    ) = take
    half = tiles // 2
    listed = send_ref.shape[0]
    per = listed // rows
    basis = slabs[0].shape[2]
    batches = groups // BATCH
    prow = lax.axis_index("prow")
    pcol = lax.axis_index("pcol")
    place = ring_place(pcol, n)
    after = ring_device((place + 1) % n, n)
    before = ring_device((place + n - 1) % n, n)
    messages = n - 1

    barrier = pltpu.get_barrier_semaphore()
    for side in (after, before):
        pl.semaphore_signal(barrier, inc=1, device_id={"pcol": side}, device_id_type=MESH)
    for d in range(1, rows):
        pl.semaphore_signal(barrier, inc=1, device_id={"prow": (prow + d) % rows}, device_id_type=MESH)

    own = [
        pltpu.make_async_copy(
            light_ref.at[:, pl.ds(o, h), pl.ds(c * basis, basis)], slabs[k].at[pl.ds(pcol * tiles, tiles)], own_sem.at[k]
        )
        for k, (c, o, h) in enumerate(chunks)
    ]
    for copy in own:
        copy.start()
    loads = [
        pltpu.make_async_copy(row_ref, row_s, index_sem.at[0]),
        pltpu.make_async_copy(col_ref, col_s, index_sem.at[1]),
        pltpu.make_async_copy(send_ref, got[0], index_sem.at[2]),
    ]
    load = pltpu.make_async_copy(blocks_ref, blk.at[pl.ds(0, count)], blk_sem)
    load_albedo = pltpu.make_async_copy(albedo_ref, alb_in, alb_sem)
    load_emission = pltpu.make_async_copy(emission_ref, out_ref, em_sem)
    pl.semaphore_wait(barrier, 2 + rows - 1)

    def piece(k, m, way, arriving):
        step = m // 2
        part = (m + way) % 2
        if way == 0:
            source = (place + n - step - arriving) % n
        else:
            source = (place + step + arriving) % n
        at = ring_device(source, n) * tiles + part * half
        window = slabs[k].at[pl.ds(at, half)]
        return pltpu.make_async_remote_copy(
            src_ref=window,
            dst_ref=window,
            send_sem=ring_send.at[way, k, m],
            recv_sem=ring_recv.at[way, k, m],
            device_id={"pcol": before if way else after},
            device_id_type=MESH,
        )

    def to_row(u, d):
        c, o, h = units[u]
        target = (prow + d) % rows
        return pltpu.make_async_remote_copy(
            src_ref=parts[c % 2].at[pl.ds(target * per, per), pl.ds(o, h)],
            dst_ref=arrived[u].at[pl.ds(prow * per, per)],
            send_sem=ex_send.at[u, d],
            recv_sem=ex_recv.at[u, d],
            device_id={"prow": target},
            device_id_type=MESH,
        )

    def from_row(u, d):
        c, o, h = units[u]
        origin = (prow + rows - d) % rows
        return pltpu.make_async_remote_copy(
            src_ref=parts[c % 2].at[pl.ds(0, per), pl.ds(o, h)],
            dst_ref=arrived[u].at[pl.ds(origin * per, per)],
            send_sem=ex_send.at[u, d],
            recv_sem=ex_recv.at[u, d],
            device_id={"prow": origin},
            device_id_type=MESH,
        )

    def stay(u):
        c, o, h = units[u]
        return pltpu.make_async_copy(
            parts[c % 2].at[pl.ds(prow * per, per), pl.ds(o, h)], arrived[u].at[pl.ds(prow * per, per)], ex_own.at[u]
        )

    def ids(d):
        return pltpu.make_async_remote_copy(
            src_ref=send_ref,
            dst_ref=got[d],
            send_sem=id_send.at[d],
            recv_sem=id_recv.at[d],
            device_id={"prow": (prow + d) % rows},
            device_id_type=MESH,
        )

    def start_loads():
        for copy in loads:
            copy.start()
        for d in range(1, rows):
            ids(d).start()
        load.start()
        load_albedo.start()
        load_emission.start()

    def make_plan():
        for copy in loads:
            copy.wait()

        def slot(s, carry):
            first, end = carry
            wanted = got[0][s]

            def narrow(_, bounds):
                low, high = bounds
                middle = (low + high) // 2
                up = jnp.logical_and(low < high, row_s[jnp.minimum(middle, count - 1)] <= wanted)
                return jnp.where(up, middle + 1, low), jnp.where(up, high, middle)

            past, _ = lax.fori_loop(0, count.bit_length(), narrow, (first, jnp.int32(count)))
            end = end + (past - first + GROUP - 1) // GROUP
            past_s[s] = past
            last_s[s] = jnp.clip(end - 1, 0, groups - 1)
            return past, end

        lax.fori_loop(0, listed, slot, (jnp.int32(0), jnp.int32(0)))
        low_col = prow * (n * tiles)

        def group(i, carry):
            s, at, keep = carry
            end = past_s[jnp.minimum(s, listed - 1)]
            for j in range(GROUP):
                inside = at + j < end
                gsrc[i * GROUP + j] = jnp.where(inside, at + j, count)
                column = col_s[jnp.minimum(at + j, count - 1)] - low_col
                gcol[i * GROUP + j] = jnp.where(inside, jnp.clip(column, 0, n * tiles - 1), 0)
            keep_s[i] = keep
            done = at + GROUP >= end
            return (
                jnp.where(done, s + 1, s),
                jnp.minimum(at + GROUP, end),
                jnp.where(done, 0, 1),
            )

        lax.fori_loop(0, groups, group, (jnp.int32(0), jnp.int32(0), jnp.int32(0)))

    def make_places():
        for d in range(1, rows):
            ids(d).wait_send()
            ids(d).wait_recv()
        low_tile = (pcol * rows + prow) * owned

        def place_of(t, carry):
            for d in range(rows):
                origin = (prow + rows - d) % rows
                at = jnp.int32(listed)
                for k in range(per):
                    at = jnp.where(got[d][prow * per + k] == low_tile + t, origin * per + k, at)
                pos_s[t * rows + d] = at
            return carry

        lax.fori_loop(0, owned, place_of, jnp.int32(0))

    def make_albedo():
        load_albedo.wait()
        alb_rows[...] = jnp.zeros(alb_rows.shape, alb_rows.dtype)
        for c in range(colours):
            for t in range(owned):
                alb_rows[pl.ds(c * owned + t, 1), :] = alb_in[pl.ds(c, 1), pl.ds(t * tile, tile)]
        alb_cols[...] = jnp.transpose(alb_rows[...])

    def pack(low, high):
        each = tile // late
        lane = lax.broadcasted_iota(jnp.int32, (tile, tile), 1)

        def one(g, carry):
            for h in range(GROUP // each):
                joined = jnp.zeros((tile, tile), blk.dtype)
                for j in range(each):
                    block = blk[gsrc[g * GROUP + h * each + j]]
                    shift = (j * late + late) % tile
                    if shift:
                        block = jnp.concatenate([block[:, tile - shift :], block[:, : tile - shift]], axis=1)
                    mine = jnp.logical_and(lane >= j * late, lane < (j + 1) * late)
                    joined = jnp.where(mine, block, joined)
                packed[g, :, pl.ds(h * tile, tile)] = joined
            return carry

        lax.fori_loop(low, high, one, jnp.int32(0))

    def full_operands(k, g):
        left, right = [], []
        for j in range(GROUP):
            left.append(blk[gsrc[g * GROUP + j]])
            lighting = slabs[k][gcol[g * GROUP + j]]
            if lighting.shape[0] < tile:
                fill = jnp.zeros((tile - lighting.shape[0], basis), lighting.dtype)
                lighting = jnp.concatenate([lighting, fill], axis=0)
            right.append(lighting)
        return jnp.concatenate(left, axis=1), jnp.concatenate(right, axis=0)

    def late_operands(k, g, o, h):
        right = [slabs[k][gcol[g * GROUP + j]] for j in range(GROUP)]
        return packed[g, pl.ds(o, h)], jnp.concatenate(right, axis=0)

    def compute(operands, batch, o, h, low, high, running):
        def one(i, running):
            products = []
            for b in range(batch):
                left, right = operands(i * batch + b)
                products.append(jnp.dot(left, right, preferred_element_type=jnp.float32))
            for b in range(batch):
                running = running * keep_s[i * batch + b].astype(jnp.float32) + products[b]
                sums[i * batch + b, pl.ds(o, h)] = running.astype(sums.dtype)
            return running

        return lax.fori_loop(low, high, one, running)

    def collect(c, o, h, add, u):
        for d in list(range(rows // 2, rows)) + list(range(rows // 2)):
            target = (prow + d) % rows
            for j in range(per):
                s = target * per + j
                value = sums[last_s[s], pl.ds(o, h)]
                if add:
                    before = parts[c % 2][s, pl.ds(o, h)]
                    value = (before.astype(jnp.float32) + value.astype(jnp.float32)).astype(sums.dtype)
                parts[c % 2][s, pl.ds(o, h)] = value
            if u is not None:
                if d:
                    to_row(u, d).start()
                else:
                    stay(u).start()

    def finish(u):
        c, o, h = units[u]
        for d in range(1, rows):
            to_row(u, d).wait_send()
            from_row(u, d).wait_recv()
        stay(u).wait()
        if u == 0:
            load_emission.wait()
        lanes = pl.ds(c * basis, basis)
        for t in range(owned):
            total = arrived[u][pos_s[t * rows]].astype(jnp.float32)
            for d in range(1, rows):
                total = total + arrived[u][pos_s[t * rows + d]].astype(jnp.float32)
            scale = alb_cols[pl.ds(o, h), pl.ds(c * owned + t, 1)]
            before = out_ref[t, pl.ds(o, h), lanes].astype(jnp.float32)
            out_ref[t, pl.ds(o, h), lanes] = (total * scale + before).astype(out_ref.dtype)

    final = len(chunks) - 1
    steps = min(messages - 1, batches)
    cuts = [batches * i // steps for i in range(steps + 1)]
    packs = [groups * i // (messages - 3) for i in range(messages - 2)]
    for k in range(len(chunks)):
        own[k].wait()
        running = jnp.zeros((tile, basis), jnp.float32)
        for m in range(messages):
            for way in (0, 1):
                if m >= 2:
                    piece(k, m - 2, way, 1).wait_recv()
                piece(k, m, way, 0).start()
            if k == 0:
                if m == 1:
                    start_loads()
                    blk[count] = jnp.zeros(blk.shape[1:], blk.dtype)
                    for buffer in arrived:
                        buffer[listed] = jnp.zeros(buffer.shape[1:], buffer.dtype)
                    make_plan()
                if m == 2:
                    make_places()
                    make_albedo()
                if m == 3:
                    load.wait()
                if m >= 3:
                    pack(packs[m - 3], packs[m - 2])
            elif m >= 1:
                if m == 1:
                    for last in range(max(messages - 2, 0), messages):
                        for way in (0, 1):
                            piece(k - 1, last, way, 1).wait_recv()
                if m <= steps:
                    operands = functools.partial(full_operands, k - 1)
                    running = compute(operands, BATCH, 0, tile, cuts[m - 1], cuts[m], running)
                if m == steps:
                    collect(chunks[k - 1][0], 0, tile, False, k - 1 if k < final else None)
                if m == max(steps - 1, 1) and k >= 2:
                    finish(k - 2)
                for way in (0, 1):
                    piece(k - 1, m, way, 0).wait_send()
                    if m == 1:
                        piece(k - 1, 0, way, 0).wait_send()
    for m in range(max(messages - 2, 0), messages):
        for way in (0, 1):
            piece(final, m, way, 1).wait_recv()
    batch = max(b * BATCH for b in (1, 2, 4) if batches % b == 0)
    for u in range(colours - 1, len(units)):
        c, o, h = units[u]
        operands = functools.partial(late_operands, final, o=o, h=h)
        compute(operands, batch, o, h, 0, groups // batch, jnp.zeros((h, basis), jnp.float32))
        collect(c, o, h, True, u)
    for m in range(messages):
        for way in (0, 1):
            piece(final, m, way, 0).wait_send()
    for u in range(colours - 1, len(units)):
        finish(u)


def write_out(from_ref, out_ref, sem):
    pieces = sem.shape[0]
    size = from_ref.shape[0] // pieces
    copies = [
        pltpu.make_async_copy(from_ref.at[pl.ds(i * size, size)], out_ref.at[pl.ds(i * size, size)], sem.at[i])
        for i in range(pieces)
    ]
    for copy in copies:
        copy.start()
    for copy in copies:
        copy.wait()


def per_device(blocks, row_index, col_index, send_tiles, lighting, albedo, emission):
    count, tile = blocks.shape[:2]
    width = lighting.shape[1]
    colours = albedo.shape[0]
    basis = width // colours
    listed = send_tiles.shape[0]
    rows = lax.axis_size("prow")
    n = lax.axis_size("pcol")
    tiles = lighting.shape[0] // tile
    owned = emission.shape[0] // tile
    groups = (count + listed * (GROUP - 1)) // GROUP
    groups = -(-groups // BATCH) * BATCH
    units = units_of(colours, tile)

    def vmem_of(late):
        tall = n * tiles * colours + (listed + 1) * colours + 2 * listed + groups
        return ((count + 1) * tile * tile + groups * tile * GROUP * late + tall * tile * basis) * 2

    late = tile // 2 if vmem_of(tile // 2) <= 58 * MIB else tile // 4
    chunks = chunks_of(colours, tile, late)
    final = len(chunks)

    hbm = pl.BlockSpec(memory_space=pltpu.HBM)
    bf16, f32, i32 = jnp.bfloat16, jnp.float32, jnp.int32
    dma = pltpu.SemaphoreType.DMA
    scratch = [pltpu.VMEM((n * tiles, h, basis), bf16) for _, _, h in chunks]
    scratch += [pltpu.VMEM((listed + 1, h, basis), bf16) for _, _, h in units]
    scratch += [pltpu.VMEM((listed, tile, basis), bf16) for _ in range(2)]
    scratch += [pltpu.SMEM((listed,), i32) for _ in range(rows)]
    scratch += [
        pltpu.VMEM((count + 1, tile, tile), bf16),
        pltpu.VMEM((groups, tile, GROUP * late), bf16),
        pltpu.VMEM((groups, tile, basis), bf16),
        pltpu.VMEM((colours, owned * tile), f32),
        pltpu.VMEM((tile, tile), f32),
        pltpu.VMEM((tile, tile), f32),
        pltpu.SMEM((count,), i32),
        pltpu.SMEM((count,), i32),
        pltpu.SMEM((listed,), i32),
        pltpu.SMEM((listed,), i32),
        pltpu.SMEM((groups * GROUP,), i32),
        pltpu.SMEM((groups * GROUP,), i32),
        pltpu.SMEM((groups,), i32),
        pltpu.SMEM((owned * rows,), i32),
        dma((2, final, n - 1)),
        dma((2, final, n - 1)),
        dma((final,)),
        dma,
        dma((3,)),
        dma,
        dma,
        dma((len(units), rows)),
        dma((len(units), rows)),
        dma((len(units),)),
        dma((rows,)),
        dma((rows,)),
    ]
    tile_bytes = tile * basis * 2
    out = pl.pallas_call(
        functools.partial(fused, n, rows, colours, groups, late),
        out_shape=pltpu.VMEM((owned, tile, width), bf16),
        in_specs=[hbm] * 7,
        out_specs=pl.BlockSpec(memory_space=pltpu.VMEM),
        scratch_shapes=scratch,
        compiler_params=pltpu.CompilerParams(
            collective_id=0, has_side_effects=True, vmem_limit_bytes=max(vmem_of(late) + MIB, 58 * MIB)
        ),
        cost_estimate=pl.CostEstimate(
            flops=2 * count * tile * tile * width,
            bytes_accessed=count * tile * tile * 2 + n * tiles * colours * tile_bytes,
            transcendentals=0,
        ),
    )(
        row_index,
        col_index,
        send_tiles,
        blocks,
        lighting.reshape(tiles, tile, width),
        albedo,
        emission.reshape(owned, tile, width),
    )
    out = pl.pallas_call(
        write_out,
        out_shape=jax.ShapeDtypeStruct((owned, tile, width), bf16),
        in_specs=[pl.BlockSpec(memory_space=pl.ANY)],
        out_specs=pl.BlockSpec(memory_space=pl.ANY),
        scratch_shapes=[dma((4,))],
        compiler_params=pltpu.CompilerParams(vmem_limit_bytes=8 * MIB),
    )(out)
    return out.reshape(owned * tile, width)


def solution(mesh):
    placed = (
        P(("prow", "pcol"), None, None),
        P(("prow", "pcol")),
        P(("prow", "pcol")),
        P(("prow", "pcol")),
        P(("prow", "pcol"), None),
        P(None, ("pcol", "prow")),
        P(("pcol", "prow"), None),
    )
    return jax.shard_map(
        per_device, mesh=mesh, in_specs=placed, out_specs=P(("pcol", "prow"), None), check_vma=False
    )
```

```python
import functools

import jax
import jax.numpy as jnp
from jax import lax
from jax.experimental import pallas as pl
from jax.experimental.pallas import tpu as pltpu
from jax.sharding import PartitionSpec as P

GROUP = 8
BATCH = 12
MIB = 1 << 20
MESH = pl.DeviceIdType.MESH


def ring_place(pcol, n):
    odd = pcol % 2
    return (1 - odd) * (pcol // 2) + odd * (n - 1 - pcol // 2)


def ring_device(place, n):
    late = place // (n // 2)
    return (1 - late) * (2 * place) + late * (2 * (n - 1 - place) + 1)


def chunks_of(colours, tile, late):
    whole = [(c, 0, tile) for c in range(colours - 1)]
    return whole + [(colours - 1, 0, tile - late), (colours - 1, tile - late, late)]


def units_of(colours, tile):
    whole = [(c, 0, tile) for c in range(colours - 1)]
    return whole + [(colours - 1, 0, tile // 2), (colours - 1, tile // 2, tile // 2)]


def fused(
    n,
    rows,
    colours,
    groups,
    late,
    row_ref,
    col_ref,
    send_ref,
    blocks_ref,
    light_ref,
    albedo_ref,
    emission_ref,
    out_ref,
    *scratch,
):
    count, tile = blocks_ref.shape[:2]
    tiles = light_ref.shape[0]
    owned = emission_ref.shape[0]
    chunks = chunks_of(colours, tile, late)
    units = units_of(colours, tile)
    take = iter(scratch)
    slabs = [next(take) for _ in chunks]
    arrived = [next(take) for _ in units]
    parts = [next(take) for _ in range(2)]
    got = [next(take) for _ in range(rows)]
    (
        blk,
        packed,
        sums,
        alb_in,
        alb_rows,
        alb_cols,
        row_s,
        col_s,
        past_s,
        last_s,
        gsrc,
        gcol,
        keep_s,
        pos_s,
        ring_send,
        ring_recv,
        own_sem,
        blk_sem,
        index_sem,
        alb_sem,
        em_sem,
        ex_send,
        ex_recv,
        ex_own,
        id_send,
        id_recv,
    ) = take
    half = tiles // 2
    listed = send_ref.shape[0]
    per = listed // rows
    basis = slabs[0].shape[2]
    batches = groups // BATCH
    prow = lax.axis_index("prow")
    pcol = lax.axis_index("pcol")
    place = ring_place(pcol, n)
    after = ring_device((place + 1) % n, n)
    before = ring_device((place + n - 1) % n, n)
    messages = n - 1

    barrier = pltpu.get_barrier_semaphore()
    for side in (after, before):
        pl.semaphore_signal(barrier, inc=1, device_id={"pcol": side}, device_id_type=MESH)
    for d in range(1, rows):
        pl.semaphore_signal(barrier, inc=1, device_id={"prow": (prow + d) % rows}, device_id_type=MESH)

    own = [
        pltpu.make_async_copy(
            light_ref.at[:, pl.ds(o, h), pl.ds(c * basis, basis)], slabs[k].at[pl.ds(pcol * tiles, tiles)], own_sem.at[k]
        )
        for k, (c, o, h) in enumerate(chunks)
    ]
    for copy in own:
        copy.start()
    loads = [
        pltpu.make_async_copy(row_ref, row_s, index_sem.at[0]),
        pltpu.make_async_copy(col_ref, col_s, index_sem.at[1]),
        pltpu.make_async_copy(send_ref, got[0], index_sem.at[2]),
    ]
    load = pltpu.make_async_copy(blocks_ref, blk.at[pl.ds(0, count)], blk_sem)
    load_albedo = pltpu.make_async_copy(albedo_ref, alb_in, alb_sem)
    load_emission = pltpu.make_async_copy(emission_ref, out_ref, em_sem)
    pl.semaphore_wait(barrier, 2 + rows - 1)

    def piece(k, m, way, arriving):
        step = m // 2
        part = (m + way) % 2
        if way == 0:
            source = (place + n - step - arriving) % n
        else:
            source = (place + step + arriving) % n
        at = ring_device(source, n) * tiles + part * half
        window = slabs[k].at[pl.ds(at, half)]
        return pltpu.make_async_remote_copy(
            src_ref=window,
            dst_ref=window,
            send_sem=ring_send.at[way, k, m],
            recv_sem=ring_recv.at[way, k, m],
            device_id={"pcol": before if way else after},
            device_id_type=MESH,
        )

    def to_row(u, d):
        c, o, h = units[u]
        target = (prow + d) % rows
        return pltpu.make_async_remote_copy(
            src_ref=parts[c % 2].at[pl.ds(target * per, per), pl.ds(o, h)],
            dst_ref=arrived[u].at[pl.ds(prow * per, per)],
            send_sem=ex_send.at[u, d],
            recv_sem=ex_recv.at[u, d],
            device_id={"prow": target},
            device_id_type=MESH,
        )

    def from_row(u, d):
        c, o, h = units[u]
        origin = (prow + rows - d) % rows
        return pltpu.make_async_remote_copy(
            src_ref=parts[c % 2].at[pl.ds(0, per), pl.ds(o, h)],
            dst_ref=arrived[u].at[pl.ds(origin * per, per)],
            send_sem=ex_send.at[u, d],
            recv_sem=ex_recv.at[u, d],
            device_id={"prow": origin},
            device_id_type=MESH,
        )

    def stay(u):
        c, o, h = units[u]
        return pltpu.make_async_copy(
            parts[c % 2].at[pl.ds(prow * per, per), pl.ds(o, h)], arrived[u].at[pl.ds(prow * per, per)], ex_own.at[u]
        )

    def ids(d):
        return pltpu.make_async_remote_copy(
            src_ref=send_ref,
            dst_ref=got[d],
            send_sem=id_send.at[d],
            recv_sem=id_recv.at[d],
            device_id={"prow": (prow + d) % rows},
            device_id_type=MESH,
        )

    def start_loads():
        for copy in loads:
            copy.start()
        for d in range(1, rows):
            ids(d).start()
        load.start()
        load_albedo.start()
        load_emission.start()

    def make_plan():
        for copy in loads:
            copy.wait()

        def slot(s, carry):
            first, end = carry
            wanted = got[0][s]

            def narrow(_, bounds):
                low, high = bounds
                middle = (low + high) // 2
                up = jnp.logical_and(low < high, row_s[jnp.minimum(middle, count - 1)] <= wanted)
                return jnp.where(up, middle + 1, low), jnp.where(up, high, middle)

            past, _ = lax.fori_loop(0, count.bit_length(), narrow, (first, jnp.int32(count)))
            end = end + (past - first + GROUP - 1) // GROUP
            past_s[s] = past
            last_s[s] = jnp.clip(end - 1, 0, groups - 1)
            return past, end

        lax.fori_loop(0, listed, slot, (jnp.int32(0), jnp.int32(0)))
        low_col = prow * (n * tiles)

        def group(i, carry):
            s, at, keep = carry
            end = past_s[jnp.minimum(s, listed - 1)]
            for j in range(GROUP):
                inside = at + j < end
                gsrc[i * GROUP + j] = jnp.where(inside, at + j, count)
                column = col_s[jnp.minimum(at + j, count - 1)] - low_col
                gcol[i * GROUP + j] = jnp.where(inside, jnp.clip(column, 0, n * tiles - 1), 0)
            keep_s[i] = keep
            done = at + GROUP >= end
            return (
                jnp.where(done, s + 1, s),
                jnp.minimum(at + GROUP, end),
                jnp.where(done, 0, 1),
            )

        lax.fori_loop(0, groups, group, (jnp.int32(0), jnp.int32(0), jnp.int32(0)))

    def make_places():
        for d in range(1, rows):
            ids(d).wait_send()
            ids(d).wait_recv()
        low_tile = (pcol * rows + prow) * owned

        def place_of(t, carry):
            for d in range(rows):
                origin = (prow + rows - d) % rows
                at = jnp.int32(listed)
                for k in range(per):
                    at = jnp.where(got[d][prow * per + k] == low_tile + t, origin * per + k, at)
                pos_s[t * rows + d] = at
            return carry

        lax.fori_loop(0, owned, place_of, jnp.int32(0))

    def make_albedo():
        load_albedo.wait()
        alb_rows[...] = jnp.zeros(alb_rows.shape, alb_rows.dtype)
        for c in range(colours):
            for t in range(owned):
                alb_rows[pl.ds(c * owned + t, 1), :] = alb_in[pl.ds(c, 1), pl.ds(t * tile, tile)]
        alb_cols[...] = jnp.transpose(alb_rows[...])

    def pack(low, high):
        each = tile // late
        lane = lax.broadcasted_iota(jnp.int32, (tile, tile), 1)

        def one(g, carry):
            for h in range(GROUP // each):
                joined = jnp.zeros((tile, tile), blk.dtype)
                for j in range(each):
                    block = blk[gsrc[g * GROUP + h * each + j]]
                    shift = (j * late + late) % tile
                    if shift:
                        block = jnp.concatenate([block[:, tile - shift :], block[:, : tile - shift]], axis=1)
                    mine = jnp.logical_and(lane >= j * late, lane < (j + 1) * late)
                    joined = jnp.where(mine, block, joined)
                packed[g, :, pl.ds(h * tile, tile)] = joined
            return carry

        lax.fori_loop(low, high, one, jnp.int32(0))

    def full_operands(k, g):
        left, right = [], []
        for j in range(GROUP):
            left.append(blk[gsrc[g * GROUP + j]])
            lighting = slabs[k][gcol[g * GROUP + j]]
            if lighting.shape[0] < tile:
                fill = jnp.zeros((tile - lighting.shape[0], basis), lighting.dtype)
                lighting = jnp.concatenate([lighting, fill], axis=0)
            right.append(lighting)
        return jnp.concatenate(left, axis=1), jnp.concatenate(right, axis=0)

    def late_operands(k, g, o, h):
        right = [slabs[k][gcol[g * GROUP + j]] for j in range(GROUP)]
        return packed[g, pl.ds(o, h)], jnp.concatenate(right, axis=0)

    def compute(operands, batch, o, h, low, high, running):
        def one(i, running):
            products = []
            for b in range(batch):
                left, right = operands(i * batch + b)
                products.append(jnp.dot(left, right, preferred_element_type=jnp.float32))
            for b in range(batch):
                running = running * keep_s[i * batch + b].astype(jnp.float32) + products[b]
                sums[i * batch + b, pl.ds(o, h)] = running.astype(sums.dtype)
            return running

        return lax.fori_loop(low, high, one, running)

    def collect(c, o, h, add, u):
        for d in list(range(rows // 2, rows)) + list(range(1, rows // 2)) + [0]:
            target = (prow + d) % rows
            for j in range(per):
                s = target * per + j
                value = sums[last_s[s], pl.ds(o, h)]
                if add:
                    before = parts[c % 2][s, pl.ds(o, h)]
                    value = (before.astype(jnp.float32) + value.astype(jnp.float32)).astype(sums.dtype)
                parts[c % 2][s, pl.ds(o, h)] = value
            if u is not None:
                if d:
                    to_row(u, d).start()
                else:
                    stay(u).start()

    def finish(u):
        c, o, h = units[u]
        for d in range(1, rows):
            to_row(u, d).wait_send()
            from_row(u, d).wait_recv()
        stay(u).wait()
        if u == 0:
            load_emission.wait()
        lanes = pl.ds(c * basis, basis)
        for t in range(owned):
            total = arrived[u][pos_s[t * rows]].astype(jnp.float32)
            for d in range(1, rows):
                total = total + arrived[u][pos_s[t * rows + d]].astype(jnp.float32)
            scale = alb_cols[pl.ds(o, h), pl.ds(c * owned + t, 1)]
            before = out_ref[t, pl.ds(o, h), lanes].astype(jnp.float32)
            out_ref[t, pl.ds(o, h), lanes] = (total * scale + before).astype(out_ref.dtype)

    final = len(chunks) - 1
    steps = min(messages - 1, batches)
    cuts = [batches * i // steps for i in range(steps + 1)]
    packs = [groups * i // (messages - 3) for i in range(messages - 2)]
    for k in range(len(chunks)):
        own[k].wait()
        running = jnp.zeros((tile, basis), jnp.float32)
        for m in range(messages):
            for way in (0, 1):
                if m >= 2:
                    piece(k, m - 2, way, 1).wait_recv()
                piece(k, m, way, 0).start()
            if k == 0:
                if m == 1:
                    start_loads()
                    blk[count] = jnp.zeros(blk.shape[1:], blk.dtype)
                    for buffer in arrived:
                        buffer[listed] = jnp.zeros(buffer.shape[1:], buffer.dtype)
                    make_plan()
                if m == 2:
                    make_places()
                    make_albedo()
                if m == 3:
                    load.wait()
                if m >= 3:
                    pack(packs[m - 3], packs[m - 2])
            elif m >= 1:
                if m == 1:
                    for last in range(max(messages - 2, 0), messages):
                        for way in (0, 1):
                            piece(k - 1, last, way, 1).wait_recv()
                if m <= steps:
                    operands = functools.partial(full_operands, k - 1)
                    running = compute(operands, BATCH, 0, tile, cuts[m - 1], cuts[m], running)
                if m == steps:
                    collect(chunks[k - 1][0], 0, tile, False, k - 1 if k < final else None)
                if m == max(steps - 1, 1) and k >= 2:
                    finish(k - 2)
                for way in (0, 1):
                    piece(k - 1, m, way, 0).wait_send()
                    if m == 1:
                        piece(k - 1, 0, way, 0).wait_send()
    for m in range(max(messages - 2, 0), messages):
        for way in (0, 1):
            piece(final, m, way, 1).wait_recv()
    batch = max(b * BATCH for b in (1, 2, 4) if batches % b == 0)
    for u in range(colours - 1, len(units)):
        c, o, h = units[u]
        operands = functools.partial(late_operands, final, o=o, h=h)
        compute(operands, batch, o, h, 0, groups // batch, jnp.zeros((h, basis), jnp.float32))
        collect(c, o, h, True, u)
    for m in range(messages):
        for way in (0, 1):
            piece(final, m, way, 0).wait_send()
    for u in range(colours - 1, len(units)):
        finish(u)


def write_out(from_ref, out_ref, sem):
    pieces = sem.shape[0]
    size = from_ref.shape[0] // pieces
    copies = [
        pltpu.make_async_copy(from_ref.at[pl.ds(i * size, size)], out_ref.at[pl.ds(i * size, size)], sem.at[i])
        for i in range(pieces)
    ]
    for copy in copies:
        copy.start()
    for copy in copies:
        copy.wait()


def per_device(blocks, row_index, col_index, send_tiles, lighting, albedo, emission):
    count, tile = blocks.shape[:2]
    width = lighting.shape[1]
    colours = albedo.shape[0]
    basis = width // colours
    listed = send_tiles.shape[0]
    rows = lax.axis_size("prow")
    n = lax.axis_size("pcol")
    tiles = lighting.shape[0] // tile
    owned = emission.shape[0] // tile
    groups = (count + listed * (GROUP - 1)) // GROUP
    groups = -(-groups // BATCH) * BATCH
    units = units_of(colours, tile)

    def vmem_of(late):
        tall = n * tiles * colours + (listed + 1) * colours + 2 * listed + groups
        return ((count + 1) * tile * tile + groups * tile * GROUP * late + tall * tile * basis) * 2

    late = tile // 2 if vmem_of(tile // 2) <= 58 * MIB else tile // 4
    chunks = chunks_of(colours, tile, late)
    final = len(chunks)

    hbm = pl.BlockSpec(memory_space=pltpu.HBM)
    bf16, f32, i32 = jnp.bfloat16, jnp.float32, jnp.int32
    dma = pltpu.SemaphoreType.DMA
    scratch = [pltpu.VMEM((n * tiles, h, basis), bf16) for _, _, h in chunks]
    scratch += [pltpu.VMEM((listed + 1, h, basis), bf16) for _, _, h in units]
    scratch += [pltpu.VMEM((listed, tile, basis), bf16) for _ in range(2)]
    scratch += [pltpu.SMEM((listed,), i32) for _ in range(rows)]
    scratch += [
        pltpu.VMEM((count + 1, tile, tile), bf16),
        pltpu.VMEM((groups, tile, GROUP * late), bf16),
        pltpu.VMEM((groups, tile, basis), bf16),
        pltpu.VMEM((colours, owned * tile), f32),
        pltpu.VMEM((tile, tile), f32),
        pltpu.VMEM((tile, tile), f32),
        pltpu.SMEM((count,), i32),
        pltpu.SMEM((count,), i32),
        pltpu.SMEM((listed,), i32),
        pltpu.SMEM((listed,), i32),
        pltpu.SMEM((groups * GROUP,), i32),
        pltpu.SMEM((groups * GROUP,), i32),
        pltpu.SMEM((groups,), i32),
        pltpu.SMEM((owned * rows,), i32),
        dma((2, final, n - 1)),
        dma((2, final, n - 1)),
        dma((final,)),
        dma,
        dma((3,)),
        dma,
        dma,
        dma((len(units), rows)),
        dma((len(units), rows)),
        dma((len(units),)),
        dma((rows,)),
        dma((rows,)),
    ]
    tile_bytes = tile * basis * 2
    out = pl.pallas_call(
        functools.partial(fused, n, rows, colours, groups, late),
        out_shape=pltpu.VMEM((owned, tile, width), bf16),
        in_specs=[hbm] * 7,
        out_specs=pl.BlockSpec(memory_space=pltpu.VMEM),
        scratch_shapes=scratch,
        compiler_params=pltpu.CompilerParams(
            collective_id=0, has_side_effects=True, vmem_limit_bytes=max(vmem_of(late) + MIB, 58 * MIB)
        ),
        cost_estimate=pl.CostEstimate(
            flops=2 * count * tile * tile * width,
            bytes_accessed=count * tile * tile * 2 + n * tiles * colours * tile_bytes,
            transcendentals=0,
        ),
    )(
        row_index,
        col_index,
        send_tiles,
        blocks,
        lighting.reshape(tiles, tile, width),
        albedo,
        emission.reshape(owned, tile, width),
    )
    out = pl.pallas_call(
        write_out,
        out_shape=jax.ShapeDtypeStruct((owned, tile, width), bf16),
        in_specs=[pl.BlockSpec(memory_space=pl.ANY)],
        out_specs=pl.BlockSpec(memory_space=pl.ANY),
        scratch_shapes=[dma((4,))],
        compiler_params=pltpu.CompilerParams(vmem_limit_bytes=8 * MIB),
    )(out)
    return out.reshape(owned * tile, width)


def solution(mesh):
    placed = (
        P(("prow", "pcol"), None, None),
        P(("prow", "pcol")),
        P(("prow", "pcol")),
        P(("prow", "pcol")),
        P(("prow", "pcol"), None),
        P(None, ("pcol", "prow")),
        P(("pcol", "prow"), None),
    )
    return jax.shard_map(
        per_device, mesh=mesh, in_specs=placed, out_specs=P(("pcol", "prow"), None), check_vma=False
    )
```
